128 devices in a mesh: row: 8 (over y_lo, x), col: 16 (over y_hi, z, core).
Axes of the slice: x: 4, y: 4 (y_hi: 2, y_lo: 2; y = y_hi * 2 + y_lo), z: 4, core: 2. Of those that a mesh axis runs over, the one named last changes fastest.
Arguments:
- acts: bfloat16 [4096, 28672], P('col', 'row'), may hold values from -6 to 6
- grads: bfloat16 [4096, 8192], P('row', 'col'), may hold values from -0.19921875 to 0.19921875
- basis_in: bfloat16 [28672, 6144], P('row', 'col'), may hold values from -0.03125 to 0.03125
- basis_out: bfloat16 [8192, 3072], P('col', 'row'), may hold values from -0.0625 to 0.0625
Outputs:
- eigenvalues: float32 [3072, 6144], P('row', 'col')
The draws below stay inside these ranges and needn't reach their ends.
All inputs are finite; a program needn't handle non-finite values.
Results may differ from the reference program's by a relative error of at most 0.0034.
Values may be sent and summed in bfloat16 or wider, within the bound.
A program may use at most 128 MiB of HBM per device.

```python
import jax
import jax.numpy as jnp

D = 8192
FF = 28672
LEN = 1024
SEQS = 4
TOKENS = 4096
KA = 6144
KG = 3072


def level_of(own_key, dims, pieces, least, high):
    loudness = 1.0
    for dim, parts in pieces:
        heights = jax.random.uniform(jax.random.fold_in(jax.random.fold_in(own_key, 6), dim), (parts,), jnp.float32, least / len(pieces), high / len(pieces))
        loudness = loudness * jnp.repeat(jnp.exp(heights), dims[dim] // parts).reshape((-1,) + (1,) * (len(dims) - 1 - dim))
    return loudness


def normal_values(rng, dims, scale, limit, cuts=(), held_as=jnp.bfloat16):
    result = scale * jax.random.normal(rng, dims, jnp.float32)
    if cuts:
        result = result * level_of(rng, dims, cuts, -0.22, 0.18)
    return jnp.clip(result, -limit, limit).astype(held_as)


def setup_inputs(seed: int = 0) -> dict:
    arg_keys = jax.random.split(jax.random.key(seed), 5)
    acts = normal_values(arg_keys[0], (TOKENS, FF), 1.0, 6.0, ((0, 16), (1, 8)))
    grads = normal_values(arg_keys[1], (TOKENS, D), 0.03, 0.19921875, ((0, 8), (1, 16)))
    basis_in = normal_values(arg_keys[2], (FF, KA), FF ** -0.5, 0.03125, ((0, 8), (1, 16)))
    basis_out = normal_values(arg_keys[3], (D, KG), D ** -0.5, 0.0625, ((0, 16), (1, 8)))
    return dict(acts=acts, grads=grads, basis_in=basis_in, basis_out=basis_out)


def reference(acts, grads, basis_in, basis_out):
    proj_in = jnp.dot(acts, basis_in, preferred_element_type=jnp.float32).astype(jnp.bfloat16)
    proj_out = jnp.dot(grads, basis_out, preferred_element_type=jnp.float32).astype(jnp.bfloat16)
    left = proj_out.reshape(SEQS, LEN, KG).astype(jnp.float32)
    right = proj_in.reshape(SEQS, LEN, KA).astype(jnp.float32)
    tile = jnp.einsum("snk,snj->skj", left, right)
    return jnp.mean(tile * tile, axis=0)
```

```python
import jax
import jax.numpy as jnp
from jax import lax
from jax.experimental import pallas as pl
from jax.experimental.pallas import tpu as pltpu
from jax.sharding import PartitionSpec as P

BF = jnp.bfloat16
F32 = jnp.float32
MESH = pl.DeviceIdType.MESH
FIRST, REST = (0, 256), (256, 128)


def kernel(
    a, b, g, h, out,
    abuf, bbuf, gbuf, hbuf,
    stg, acc, rx, lst, lrx, pin,
    zst, zacc, zrx, hst, hrx, pout,
    est, erx,
    loc, ss, rs, xs, xr, ls, lr, ps, pr, gs, gr, zs, zr, es, er,
):
    row, col = lax.axis_index("row"), lax.axis_index("col")
    lo, x = row // 4, row % 4
    c, z, hi = col % 2, (col // 2) % 4, col // 8
    p, z0 = z // 2, z % 2
    rows = a.shape[0]
    half = rows // 2
    depth = h.shape[0]
    kb = b.shape[1]

    def dev(x=x, lo=lo, hi=hi, z=z, c=c):
        return (lo * 4 + x, (hi * 4 + z) * 2 + c)

    d_y = dev(hi=1 - hi)
    d_z = dev(z=z + 1 - 2 * z0)
    d_q = dev(z=3 - z)
    d_c = dev(c=1 - c)
    d_l = dev(lo=1 - lo)
    d_d = dev(lo=1 - lo, z=3 - z)
    d_x = [dev(x=(x + r) % 4) for r in (1, 2, 3)]
    d_2 = dev(z=(z + 2) % 4)

    pending = []

    def copy(src, dst, send, recv, to):
        return pltpu.make_async_remote_copy(
            src_ref=src, dst_ref=dst, send_sem=send, recv_sem=recv, device_id=to, device_id_type=MESH
        )

    def send(src, dst, i, to):
        cp = copy(src, dst, ss.at[i], rs.at[i], to)
        cp.start()
        pending.append(cp)

    def got(dst, i):
        copy(dst, dst, ss.at[i], rs.at[i], d_c).wait_recv()

    own = hi * 4 + z0 * 2 + c
    i_y = (1 - hi) * 4 + z0 * 2 + c
    i_z = hi * 4 + (1 - z0) * 2 + c
    i_d = (1 - hi) * 4 + (1 - z0) * 2 + c

    def sib(i):
        return i + 1 - 2 * c

    top, low = pl.ds(0, half), pl.ds(half, half)
    mine = pl.ds(pl.multiple_of(c * depth, depth), depth)
    other = pl.ds(pl.multiple_of((1 - c) * depth, depth), depth)
    l_a = pltpu.make_async_copy(a, abuf.at[own], loc.at[0])
    l_b = pltpu.make_async_copy(b, bbuf.at[p], loc.at[1])
    l_g = pltpu.make_async_copy(g.at[pl.ds(pl.multiple_of(c * rows, rows), rows)], gbuf.at[x, :, mine], loc.at[2])
    l_h = pltpu.make_async_copy(h, hbuf.at[lo, mine], loc.at[3])
    for cp in (l_g, l_a, l_b, l_h):
        cp.start()

    barrier = pltpu.get_barrier_semaphore()
    friends = [d_y, d_z, d_q, d_c, d_l, d_d, d_2] + d_x
    for to in friends:
        pl.semaphore_signal(barrier, inc=1, device_id=to, device_id_type=MESH)
    pl.semaphore_wait(barrier, len(friends))

    send(g.at[pl.ds(pl.multiple_of((1 - c) * rows, rows), rows)], gbuf.at[x, :, mine], 3, d_c)
    send(a.at[top], abuf.at[own, top], 0, d_y)
    send(a.at[low], abuf.at[own, low], 1, d_z)
    send(b.at[:, pl.ds(*FIRST)], bbuf.at[p, :, pl.ds(*FIRST)], 2, d_q)
    send(a, abuf.at[own], 6, d_c)
    send(h, hbuf.at[lo, mine], 4, d_c)
    send(h, hbuf.at[lo, mine], 5, d_l)
    send(a.at[low], abuf.at[own, low], 7, d_y)
    send(a.at[top], abuf.at[own, top], 8, d_z)
    send(b.at[:, pl.ds(*REST)], bbuf.at[p, :, pl.ds(*REST)], 9, d_q)

    l_g.wait()
    got(gbuf.at[x, :, other], 3)
    for r in (1, 2, 3):
        cp = copy(gbuf.at[x], gbuf.at[x], gs.at[r - 1], gr.at[r - 1], d_x[r - 1])
        cp.start()
        pending.append(cp)

    def x_copy(idx, pb, cols, ch):
        to = idx % 4
        rel = (x - to + 4) % 4
        s = (idx // 4, jnp.maximum(rel, 1) - 1, pb, slice(None), pl.ds(*cols))
        return copy(
            stg.at[idx, pb, :, pl.ds(*cols)], rx.at[s], xs.at[idx, ch], xr.at[idx // 4, jnp.maximum(rel, 1) - 1, ch], dev(x=to)
        )

    def block(idx, pb, cols, ch):
        part = jnp.dot(abuf[idx], bbuf[pb, :, pl.ds(*cols)], preferred_element_type=F32)

        @pl.when(idx % 4 == x)
        def _():
            acc[idx // 4, pb, :, pl.ds(*cols)] = part

        @pl.when(idx % 4 != x)
        def _():
            stg[idx, pb, :, pl.ds(*cols)] = part.astype(BF)
            x_copy(idx, pb, cols, ch).start()

    full = (0, kb)
    l_a.wait()
    l_b.wait()
    got(abuf.at[sib(own)], 6)

    @pl.loop(0, 2)
    def _(j):
        block(hi * 4 + z0 * 2 + (c + j) % 2, p, full, 0)

    got(abuf.at[i_y, top], 0)
    send(abuf.at[i_y, top], abuf.at[i_y, top], 10, d_z)
    send(abuf.at[i_y, top], abuf.at[i_y, top], 11, d_c)
    got(abuf.at[i_z, low], 1)
    send(abuf.at[i_z, low], abuf.at[i_z, low], 12, d_y)
    send(abuf.at[i_z, low], abuf.at[i_z, low], 13, d_c)

    l_h.wait()
    got(hbuf.at[1 - lo, mine], 5)
    send(hbuf.at[1 - lo, mine], hbuf.at[1 - lo, mine], 14, d_c)
    got(hbuf.at[lo, other], 4)
    for r in (1, 2, 3):
        src = (x + 4 - r) % 4
        copy(gbuf.at[src], gbuf.at[src], gs.at[r - 1], gr.at[r - 1], d_x[r - 1]).wait_recv()
    got(hbuf.at[1 - lo, other], 14)

    def z_copy(t):
        rel = jnp.maximum((z - t + 4) % 4, 1) - 1
        return copy(zst.at[t], zrx.at[rel], zs.at[t], zr.at[rel], dev(z=t))

    @pl.loop(0, 4)
    def _(t):
        for k in (0, 1):
            part = jnp.dot(gbuf[t], hbuf[k], preferred_element_type=F32)

            @pl.when(t == z)
            def _():
                zacc[k] = part

            @pl.when(t != z)
            def _():
                zst[t, k] = part.astype(zst.dtype)

        @pl.when(t != z)
        def _():
            z_copy(t).start()

    got(abuf.at[i_y, low], 7)
    send(abuf.at[i_y, low], abuf.at[i_y, low], 15, d_c)
    got(abuf.at[i_z, top], 8)
    send(abuf.at[i_z, top], abuf.at[i_z, top], 16, d_c)
    got(abuf.at[sib(i_y), top], 11)
    got(abuf.at[sib(i_z), low], 13)
    got(abuf.at[sib(i_y), low], 15)
    got(abuf.at[sib(i_z), top], 16)

    def near(j):
        k = j // 2
        h_ = jnp.where(k == 1, 1 - hi, hi)
        z_ = jnp.where(k == 2, 1 - z0, z0)
        return h_ * 4 + z_ * 2 + (c + j) % 2

    @pl.loop(2, 6)
    def _(j):
        block(near(j), p, full, 0)

    got(bbuf.at[1 - p, :, pl.ds(*FIRST)], 2)

    @pl.loop(0, 6)
    def _(j):
        block(near(j), 1 - p, FIRST, 1)

    got(abuf.at[i_d, top], 10)
    send(abuf.at[i_d, top], abuf.at[i_d, top], 17, d_c)
    got(abuf.at[i_d, low], 12)
    send(abuf.at[i_d, low], abuf.at[i_d, low], 18, d_c)
    got(bbuf.at[1 - p, :, pl.ds(*REST)], 9)
    got(abuf.at[sib(i_d), top], 17)
    got(abuf.at[sib(i_d), low], 18)

    @pl.loop(0, 2)
    def _(j):
        idx = (1 - hi) * 4 + (1 - z0) * 2 + (c + j) % 2
        block(idx, p, full, 0)
        block(idx, 1 - p, FIRST, 1)
        block(idx, 1 - p, REST, 2)

    @pl.loop(0, 6)
    def _(j):
        block(near(j), 1 - p, REST, 2)

    for r in (1, 2, 3):
        copy(zst.at[0], zrx.at[r - 1], zs.at[0], zr.at[r - 1], d_c).wait_recv()
    for k in (0, 1):
        zacc[k] = zacc[k] + zrx[0, k].astype(F32) + zrx[1, k].astype(F32) + zrx[2, k].astype(F32)
        hst[k] = zacc[k].astype(hst.dtype)
    send(hst, hrx, 19, d_y)

    pieces = ((p, full), (1 - p, FIRST), (1 - p, REST))
    for ch, (pb, cols) in enumerate(pieces):
        cs = pl.ds(*cols)
        for k, hh in enumerate((1 - lo, lo)):
            for r in range(3):
                ref = rx.at[hh, r, pb, :, cs]
                copy(ref, ref, xs.at[0, ch], xr.at[hh, r, ch], d_c).wait_recv()
            total = acc[hh, pb, :, cs]
            for r in range(3):
                total = total + rx[hh, r, pb, :, cs].astype(F32)
            if k == 0:
                lst[pb, :, cs] = total.astype(lst.dtype)
                cp = copy(lst.at[pb, :, cs], lrx.at[pb, :, cs], ls.at[ch], lr.at[ch], d_l)
                cp.start()
                pending.append(cp)
            else:
                acc[hh, pb, :, cs] = total

    got(hrx, 19)
    at = pl.ds(pl.multiple_of((z0 * 2 + c) * rows, rows), rows)
    at_c = pl.ds(pl.multiple_of((z0 * 2 + 1 - c) * rows, rows), rows)
    at_z = pl.ds(pl.multiple_of(((1 - z0) * 2 + c) * rows, rows), rows)
    at_d = pl.ds(pl.multiple_of(((1 - z0) * 2 + 1 - c) * rows, rows), rows)
    for k in (0, 1):
        pout[k, at] = (zacc[k] + hrx[k].astype(F32)).astype(BF)
    send(pout.at[:, at], pout.at[:, at], 20, d_z)
    send(pout.at[:, at], pout.at[:, at], 21, d_c)

    here = pl.ds(pl.multiple_of(x * rows, rows), rows)
    for ch, (pb, cols) in enumerate(pieces):
        cs = pl.ds(*cols)
        ref = lrx.at[pb, :, cs]
        copy(ref, ref, ls.at[ch], lr.at[ch], d_l).wait_recv()
        pin[pb, here, cs] = (acc[lo, pb, :, cs] + lrx[pb, :, cs].astype(F32)).astype(BF)
        for r in (1, 2, 3):
            ref = pin.at[pb, here, cs]
            cp = copy(ref, ref, ps.at[ch, r - 1], pr.at[ch, r - 1], d_x[r - 1])
            cp.start()
            pending.append(cp)

    got(pout.at[:, at_z], 20)
    send(pout.at[:, at_z], pout.at[:, at_z], 22, d_c)
    got(pout.at[:, at_c], 21)
    got(pout.at[:, at_d], 22)
    for ch, (pb, cols) in enumerate(pieces):
        for r in (1, 2, 3):
            src = pl.ds(pl.multiple_of((x + 4 - r) % 4 * rows, rows), rows)
            ref = pin.at[pb, src, pl.ds(*cols)]
            copy(ref, ref, ps.at[ch, r - 1], pr.at[ch, r - 1], d_c).wait_recv()

    def squares(k, pb):
        t = lax.dot_general(pout[k], pin[pb], (((0,), (0,)), ((), ())), preferred_element_type=F32)
        return t * t

    for i, (k, pb, to) in enumerate(((1 - lo, 1 - p, d_d), (1 - lo, p, d_l), (lo, 1 - p, d_q))):
        est[i] = squares(k, pb).astype(est.dtype)
        cp = copy(est.at[i], erx.at[i], es.at[i], er.at[i], to)
        cp.start()
        pending.append(cp)
    total = squares(lo, p)
    for i in range(3):
        copy(erx.at[i], erx.at[i], es.at[i], er.at[i], d_c).wait_recv()
        total = total + erx[i].astype(F32)
    out[...] = total * 0.25

    for cp in pending:
        cp.wait_send()

    @pl.loop(0, 8)
    def _(idx):
        @pl.when(idx % 4 != x)
        def _():
            for ch, (pb, cols) in enumerate(pieces):
                x_copy(idx, pb, cols, ch).wait_send()

    @pl.loop(0, 4)
    def _(t):
        @pl.when(t != z)
        def _():
            z_copy(t).wait_send()


def per_device(acts, grads, basis_in, basis_out):
    rows, feats = acts.shape
    kb = basis_in.shape[1]
    depth, kg = basis_out.shape
    dma = pltpu.SemaphoreType.DMA
    return pl.pallas_call(
        kernel,
        out_shape=jax.ShapeDtypeStruct((kg, kb), F32),
        in_specs=[pl.BlockSpec(memory_space=pl.ANY)] * 4,
        out_specs=pl.BlockSpec(memory_space=pltpu.VMEM),
        scratch_shapes=[
            pltpu.VMEM((8, rows, feats), BF),
            pltpu.VMEM((2, feats, kb), BF),
            pltpu.VMEM((4, rows, 2 * depth), BF),
            pltpu.VMEM((2, 2 * depth, kg), BF),
            pltpu.VMEM((8, 2, rows, kb), BF),
            pltpu.VMEM((2, 2, rows, kb), F32),
            pltpu.VMEM((2, 3, 2, rows, kb), BF),
            pltpu.VMEM((2, rows, kb), BF),
            pltpu.VMEM((2, rows, kb), BF),
            pltpu.VMEM((2, 4 * rows, kb), BF),
            pltpu.VMEM((4, 2, rows, kg), BF),
            pltpu.VMEM((2, rows, kg), F32),
            pltpu.VMEM((3, 2, rows, kg), BF),
            pltpu.VMEM((2, rows, kg), F32),
            pltpu.VMEM((2, rows, kg), F32),
            pltpu.VMEM((2, 4 * rows, kg), BF),
            pltpu.VMEM((3, kg, kb), BF),
            pltpu.VMEM((3, kg, kb), BF),
            dma((4,)),
            dma((23,)), dma((23,)),
            dma((8, 3)), dma((2, 3, 3)),
            dma((3,)), dma((3,)),
            dma((3, 3)), dma((3, 3)),
            dma((3,)), dma((3,)),
            dma((4,)), dma((3,)),
            dma((3,)), dma((3,)),
        ],
        compiler_params=pltpu.CompilerParams(
            collective_id=0, has_side_effects=True, vmem_limit_bytes=58 * 2**20
        ),
        cost_estimate=pl.CostEstimate(flops=14 * 10**9, bytes_accessed=7 * 10**6, transcendentals=0),
    )(acts, basis_in, grads, basis_out)


def solution(mesh):
    in_specs = (P("col", "row"), P("row", "col"), P("row", "col"), P("col", "row"))
    return jax.shard_map(
        per_device, mesh=mesh, in_specs=in_specs, out_specs=P("row", "col"), check_vma=False
    )
```

```python
import jax
import jax.numpy as jnp
from jax import lax
from jax.experimental import pallas as pl
from jax.experimental.pallas import tpu as pltpu
from jax.sharding import PartitionSpec as P

BF = jnp.bfloat16
F32 = jnp.float32
MESH = pl.DeviceIdType.MESH
FIRST, REST = (0, 256), (256, 128)


def kernel(
    a, b, g, h, out,
    abuf, bbuf, gbuf, hbuf,
    cf, stg, acc, rx, lst, lrx, pin,
    zst, zacc, zrx, hst, hrx, pout,
    est, erx,
    loc, ss, rs, xs, xr, ls, lr, ps, pr, gs, gr, zs, zr, es, er,
):
    row, col = lax.axis_index("row"), lax.axis_index("col")
    lo, x = row // 4, row % 4
    c, z, hi = col % 2, (col // 2) % 4, col // 8
    p, z0 = z // 2, z % 2
    rows, feats = a.shape
    half = rows // 2
    part_rows = rows // 4
    depth, kg = h.shape
    kb = b.shape[1]

    def dev(x=x, lo=lo, hi=hi, z=z, c=c):
        return (lo * 4 + x, (hi * 4 + z) * 2 + c)

    d_y = dev(hi=1 - hi)
    d_z = dev(z=z + 1 - 2 * z0)
    d_q = dev(z=3 - z)
    d_c = dev(c=1 - c)
    d_l = dev(lo=1 - lo)
    d_d = dev(lo=1 - lo, z=3 - z)
    d_x = [dev(x=(x + r) % 4) for r in (1, 2, 3)]
    d_2 = dev(z=(z + 2) % 4)

    pending = []

    def copy(src, dst, send, recv, to):
        return pltpu.make_async_remote_copy(
            src_ref=src, dst_ref=dst, send_sem=send, recv_sem=recv, device_id=to, device_id_type=MESH
        )

    def start(cp):
        cp.start()
        pending.append(cp)

    def send(src, dst, i, to):
        start(copy(src, dst, ss.at[i], rs.at[i], to))

    def got(dst, i):
        copy(dst, dst, ss.at[i], rs.at[i], d_c).wait_recv()

    s_o = hi * 2 + z0
    s_y = (1 - hi) * 2 + z0
    s_z = hi * 2 + 1 - z0
    s_d = (1 - hi) * 2 + 1 - z0
    top, low = pl.ds(0, half), pl.ds(half, half)
    mine = pl.ds(pl.multiple_of(c * depth, depth), depth)
    other = pl.ds(pl.multiple_of((1 - c) * depth, depth), depth)
    l_a = [pltpu.make_async_copy(a.at[pl.ds(k * half, half)], abuf.at[s_o, k, c], loc.at[k]) for k in (0, 1)]
    l_b = pltpu.make_async_copy(b, bbuf.at[p], loc.at[2])
    l_g = pltpu.make_async_copy(g.at[pl.ds(pl.multiple_of(c * rows, rows), rows)], gbuf.at[x, :, mine], loc.at[3])
    l_h = pltpu.make_async_copy(h, hbuf.at[lo, mine], loc.at[4])
    for cp in (l_g, l_h, *l_a, l_b):
        cp.start()

    barrier = pltpu.get_barrier_semaphore()
    friends = [d_y, d_z, d_q, d_c, d_l, d_d, d_2] + d_x
    for to in friends:
        pl.semaphore_signal(barrier, inc=1, device_id=to, device_id_type=MESH)
    pl.semaphore_wait(barrier, len(friends))

    send(g.at[pl.ds(pl.multiple_of((1 - c) * rows, rows), rows)], gbuf.at[x, :, mine], 0, d_c)
    send(h, hbuf.at[lo, mine], 1, d_l)
    send(a.at[top], abuf.at[s_o, 0, c], 2, d_y)
    send(a.at[low], abuf.at[s_o, 1, c], 3, d_z)
    send(b.at[:, pl.ds(*FIRST)], bbuf.at[p, :, pl.ds(*FIRST)], 4, d_q)
    send(a.at[top], abuf.at[s_o, 0, c], 5, d_c)
    send(a.at[low], abuf.at[s_o, 1, c], 6, d_c)
    send(h, hbuf.at[lo, mine], 7, d_c)
    send(a.at[low], abuf.at[s_o, 1, c], 8, d_y)
    send(a.at[top], abuf.at[s_o, 0, c], 9, d_z)
    send(b.at[:, pl.ds(*REST)], bbuf.at[p, :, pl.ds(*REST)], 10, d_q)

    l_g.wait()
    got(gbuf.at[x, :, other], 0)
    for r in (1, 2, 3):
        start(copy(gbuf.at[x], gbuf.at[x], gs.at[r - 1], gr.at[r - 1], d_x[r - 1]))

    def x_copy(s, k, pb, cols, ch, r):
        cs = pl.ds(*cols)
        quarter = pl.ds(pl.multiple_of((x + r) % 4 * part_rows, part_rows), part_rows)
        u = s * 2 + k
        return copy(
            stg.at[s, k, pb, quarter, cs], rx.at[r - 1, s, k, pb, :, cs], xs.at[u, ch, r - 1], xr.at[u, ch, r - 1], d_x[r - 1]
        )

    full = (0, kb)
    kept = pl.ds(pl.multiple_of(x * part_rows, part_rows), part_rows)

    def block(s, k, pb, cols, chunks):
        cs = pl.ds(*cols)
        lhs = abuf[s, k].reshape(rows, feats)
        part = jnp.dot(lhs, bbuf[pb, :, cs], preferred_element_type=F32)
        cf[:, cs] = part
        stg[s, k, pb, :, cs] = part.astype(BF)
        for ch, piece in chunks:
            for r in (1, 2, 3):
                x_copy(s, k, pb, piece, ch, r).start()
        acc[s, k, pb, :, cs] = cf[kept, cs]

    def first(s, k):
        block(s, k, p, full, [(0, full)])

    for cp in l_a:
        cp.wait()
    l_b.wait()
    got(abuf.at[s_o, 0, 1 - c], 5)
    got(abuf.at[s_o, 1, 1 - c], 6)

    @pl.loop(0, 2)
    def _(k):
        first(s_o, k)

    got(abuf.at[s_y, 0, c], 2)
    send(abuf.at[s_y, 0, c], abuf.at[s_y, 0, c], 11, d_c)
    got(abuf.at[s_z, 1, c], 3)
    send(abuf.at[s_z, 1, c], abuf.at[s_z, 1, c], 12, d_c)
    got(hbuf.at[1 - lo, mine], 1)
    send(hbuf.at[1 - lo, mine], hbuf.at[1 - lo, mine], 13, d_c)
    got(abuf.at[s_y, 0, 1 - c], 11)
    got(abuf.at[s_z, 1, 1 - c], 12)

    @pl.loop(0, 2)
    def _(k):
        first(jnp.where(k == 0, s_y, s_z), k)

    l_h.wait()
    got(hbuf.at[lo, other], 7)
    got(hbuf.at[1 - lo, other], 13)
    for r in (1, 2, 3):
        src = (x + 4 - r) % 4
        copy(gbuf.at[src], gbuf.at[src], gs.at[r - 1], gr.at[r - 1], d_c).wait_recv()

    def z_copy(t):
        rel = jnp.maximum((z - t + 4) % 4, 1) - 1
        return copy(zst.at[t], zrx.at[rel], zs.at[t], zr.at[rel], dev(z=t))

    @pl.loop(0, 4)
    def _(t):
        for k in (0, 1):
            part = jnp.dot(gbuf[t], hbuf[k], preferred_element_type=F32)

            @pl.when(t == z)
            def _():
                zacc[k] = part

            @pl.when(t != z)
            def _():
                zst[t, k] = part.astype(zst.dtype)

        @pl.when(t != z)
        def _():
            z_copy(t).start()

    got(abuf.at[s_y, 1, c], 8)
    send(abuf.at[s_z, 1, c], abuf.at[s_z, 1, c], 15, d_y)
    send(abuf.at[s_y, 1, c], abuf.at[s_y, 1, c], 16, d_c)
    got(abuf.at[s_z, 0, c], 9)
    send(abuf.at[s_y, 0, c], abuf.at[s_y, 0, c], 14, d_z)
    send(abuf.at[s_z, 0, c], abuf.at[s_z, 0, c], 17, d_c)
    got(abuf.at[s_y, 1, 1 - c], 16)
    got(abuf.at[s_z, 0, 1 - c], 17)

    @pl.loop(0, 2)
    def _(k):
        first(jnp.where(k == 0, s_z, s_y), k)

    got(bbuf.at[1 - p, :, pl.ds(*FIRST)], 4)

    def near(j):
        return jnp.where(j < 2, s_o, jnp.where(j < 4, s_y, s_z))

    @pl.loop(0, 6)
    def _(j):
        block(near(j), j % 2, 1 - p, FIRST, [(1, FIRST)])

    def add_x(zz, pb, cols, chunks, i):
        cs = pl.ds(*cols)
        for hh in (1 - lo, lo):
            s = hh * 2 + zz
            for k in (0, 1):
                for ch, piece in chunks:
                    for r in range(3):
                        ref = rx.at[r, s, k, pb, :, pl.ds(*piece)]
                        copy(ref, ref, xs.at[0, 0, 0], xr.at[s * 2 + k, ch, r], d_c).wait_recv()
            total = acc[s, :, pb, :, cs]
            for r in range(3):
                total = total + rx[r, s, :, pb, :, cs].astype(F32)
            if hh is lo:
                acc[s, :, pb, :, cs] = total
            else:
                lst[zz, :, pb, :, cs] = total.astype(lst.dtype)
                start(copy(lst.at[zz, :, pb, :, cs], lrx.at[zz, :, pb, :, cs], ls.at[i], lr.at[i], d_l))

    def add_y(zz, pb, cols, i):
        cs = pl.ds(*cols)
        ref = lrx.at[zz, :, pb, :, cs]
        copy(ref, ref, ls.at[i], lr.at[i], d_c).wait_recv()
        pin[pb, zz, :, x, :, cs] = (acc[lo * 2 + zz, :, pb, :, cs] + lrx[zz, :, pb, :, cs].astype(F32)).astype(BF)
        for r in (1, 2, 3):
            ref = pin.at[pb, zz, :, x, :, cs]
            start(copy(ref, ref, ps.at[i, r - 1], pr.at[i, r - 1], d_x[r - 1]))

    def gathered(zz, pb, cols, i):
        for r in (1, 2, 3):
            ref = pin.at[pb, zz, :, (x + 4 - r) % 4, :, pl.ds(*cols)]
            copy(ref, ref, ps.at[i, r - 1], pr.at[i, r - 1], d_c).wait_recv()

    add_x(z0, p, full, [(0, full)], 0)
    add_x(z0, 1 - p, FIRST, [(1, FIRST)], 1)

    got(bbuf.at[1 - p, :, pl.ds(*REST)], 10)

    @pl.loop(0, 6)
    def _(j):
        block(near(j), j % 2, 1 - p, REST, [(2, REST)])

    for r in (1, 2, 3):
        copy(zst.at[0], zrx.at[r - 1], zs.at[0], zr.at[r - 1], d_c).wait_recv()
    for k in (0, 1):
        zacc[k] = zacc[k] + zrx[0, k].astype(F32) + zrx[1, k].astype(F32) + zrx[2, k].astype(F32)
        hst[k] = zacc[k].astype(hst.dtype)
    send(hst, hrx, 18, d_y)

    add_y(z0, p, full, 0)
    add_y(z0, 1 - p, FIRST, 1)

    got(abuf.at[s_d, 0, c], 14)
    send(abuf.at[s_d, 0, c], abuf.at[s_d, 0, c], 19, d_c)
    got(abuf.at[s_d, 1, c], 15)
    send(abuf.at[s_d, 1, c], abuf.at[s_d, 1, c], 20, d_c)
    got(abuf.at[s_d, 0, 1 - c], 19)
    got(abuf.at[s_d, 1, 1 - c], 20)

    @pl.loop(0, 2)
    def _(k):
        first(s_d, k)

    @pl.loop(0, 2)
    def _(k):
        block(s_d, k, 1 - p, full, [(1, FIRST), (2, REST)])

    add_x(1 - z0, p, full, [(0, full)], 2)
    add_x(z0, 1 - p, REST, [(2, REST)], 3)
    add_x(1 - z0, 1 - p, full, [(1, FIRST), (2, REST)], 4)
    add_y(1 - z0, p, full, 2)
    add_y(z0, 1 - p, REST, 3)
    add_y(1 - z0, 1 - p, full, 4)

    got(hrx, 18)
    for k in (0, 1):
        pout[k, z0, :, c] = (zacc[k] + hrx[k].astype(F32)).astype(BF).reshape(2, half, kg)
    send(pout.at[:, z0, :, c], pout.at[:, z0, :, c], 21, d_z)
    send(pout.at[:, z0, :, c], pout.at[:, z0, :, c], 22, d_c)
    got(pout.at[:, 1 - z0, :, c], 21)
    send(pout.at[:, 1 - z0, :, c], pout.at[:, 1 - z0, :, c], 23, d_c)
    got(pout.at[:, z0, :, 1 - c], 22)
    got(pout.at[:, 1 - z0, :, 1 - c], 23)

    def squares(k, pb):
        left = pout[k].reshape(4 * rows, kg)
        right = pin[pb].reshape(4 * rows, kb)
        t = lax.dot_general(left, right, (((0,), (0,)), ((), ())), preferred_element_type=F32)
        return t * t

    def give(i, k, pb, to):
        est[i] = squares(k, pb).astype(est.dtype)
        start(copy(est.at[i], erx.at[i], es.at[i], er.at[i], to))

    gathered(z0, p, full, 0)
    gathered(1 - z0, p, full, 2)
    give(0, 1 - lo, p, d_l)
    gathered(z0, 1 - p, FIRST, 1)
    gathered(z0, 1 - p, REST, 3)
    gathered(1 - z0, 1 - p, full, 4)
    give(1, 1 - lo, 1 - p, d_d)
    give(2, lo, 1 - p, d_q)
    total = squares(lo, p)
    for i in range(3):
        copy(erx.at[i], erx.at[i], es.at[i], er.at[i], d_c).wait_recv()
        total = total + erx[i].astype(F32)
    out[...] = total * 0.25

    for cp in pending:
        cp.wait_send()

    @pl.loop(0, 8)
    def _(u):
        for ch, (pb, piece) in enumerate(((p, full), (1 - p, FIRST), (1 - p, REST))):
            for r in (1, 2, 3):
                x_copy(u // 2, u % 2, pb, piece, ch, r).wait_send()

    @pl.loop(0, 4)
    def _(t):
        @pl.when(t != z)
        def _():
            z_copy(t).wait_send()


def per_device(acts, grads, basis_in, basis_out):
    rows, feats = acts.shape
    kb = basis_in.shape[1]
    depth, kg = basis_out.shape
    dma = pltpu.SemaphoreType.DMA
    return pl.pallas_call(
        kernel,
        out_shape=jax.ShapeDtypeStruct((kg, kb), F32),
        in_specs=[pl.BlockSpec(memory_space=pl.ANY)] * 4,
        out_specs=pl.BlockSpec(memory_space=pltpu.VMEM),
        scratch_shapes=[
            pltpu.VMEM((4, 2, 2, rows // 2, feats), BF),
            pltpu.VMEM((2, feats, kb), BF),
            pltpu.VMEM((4, rows, 2 * depth), BF),
            pltpu.VMEM((2, 2 * depth, kg), BF),
            pltpu.VMEM((rows, kb), F32),
            pltpu.VMEM((4, 2, 2, rows, kb), BF),
            pltpu.VMEM((4, 2, 2, rows // 4, kb), F32),
            pltpu.VMEM((3, 4, 2, 2, rows // 4, kb), BF),
            pltpu.VMEM((2, 2, 2, rows // 4, kb), BF),
            pltpu.VMEM((2, 2, 2, rows // 4, kb), BF),
            pltpu.VMEM((2, 2, 2, 4, rows // 4, kb), BF),
            pltpu.VMEM((4, 2, rows, kg), BF),
            pltpu.VMEM((2, rows, kg), F32),
            pltpu.VMEM((3, 2, rows, kg), BF),
            pltpu.VMEM((2, rows, kg), F32),
            pltpu.VMEM((2, rows, kg), F32),
            pltpu.VMEM((2, 2, 2, 2, rows // 2, kg), BF),
            pltpu.VMEM((3, kg, kb), BF),
            pltpu.VMEM((3, kg, kb), BF),
            dma((5,)),
            dma((24,)), dma((24,)),
            dma((8, 3, 3)), dma((8, 3, 3)),
            dma((5,)), dma((5,)),
            dma((5, 3)), dma((5, 3)),
            dma((3,)), dma((3,)),
            dma((4,)), dma((3,)),
            dma((3,)), dma((3,)),
        ],
        compiler_params=pltpu.CompilerParams(
            collective_id=0, has_side_effects=True, vmem_limit_bytes=58 * 2**20
        ),
        cost_estimate=pl.CostEstimate(flops=14 * 10**9, bytes_accessed=7 * 10**6, transcendentals=0),
    )(acts, basis_in, grads, basis_out)


def solution(mesh):
    in_specs = (P("col", "row"), P("row", "col"), P("row", "col"), P("col", "row"))
    return jax.shard_map(
        per_device, mesh=mesh, in_specs=in_specs, out_specs=P("row", "col"), check_vma=False
    )
```

```python
import jax
import jax.numpy as jnp
from jax import lax
from jax.experimental import pallas as pl
from jax.experimental.pallas import tpu as pltpu
from jax.sharding import PartitionSpec as P

BF = jnp.bfloat16
F32 = jnp.float32
MESH = pl.DeviceIdType.MESH
OWN, FIRST, REST = (0, 0, 384), (1, 0, 256), (1, 256, 128)
PIECES = (OWN, FIRST, REST)
TOP, LOW, THIRD, FOURTH, ALL = (0, 2), (2, 2), (2, 1), (3, 1), (0, 4)
MESSAGES = {TOP: [TOP], LOW: [THIRD, FOURTH], THIRD: [THIRD], FOURTH: [FOURTH], ALL: [TOP, THIRD, FOURTH]}


def kernel(
    a, b, g, h, out,
    abuf, bbuf, gbuf, hbuf,
    cf, stg, acc, rx, lst, lrx, pin,
    zst, zall, zrx, pout,
    est, erx, esum,
    loc, ss, rs, xs, xr, ls, lr, ps, pr, gs, gr, zs, zr, es, er,
):
    row, col = lax.axis_index("row"), lax.axis_index("col")
    lo, x = row // 4, row % 4
    c, z, hi = col % 2, (col // 2) % 4, col // 8
    z0 = z % 2
    rows, feats = a.shape
    qr = rows // 4
    xrows = 2 * qr // 4
    depth, kg = h.shape
    kb = b.shape[1]

    def dev(x=x, lo=lo, hi=hi, z=z, c=c):
        return (lo * 4 + x, (hi * 4 + z) * 2 + c)

    d_y = dev(hi=1 - hi)
    d_z = dev(z=z + 1 - 2 * z0)
    d_q = dev(z=3 - z)
    d_c = dev(c=1 - c)
    d_yc = dev(hi=1 - hi, c=1 - c)
    d_l = dev(lo=1 - lo)
    d_b = dev(lo=1 - lo, hi=1 - hi)
    d_x = [dev(x=(x + r) % 4) for r in (1, 2, 3)]
    d_zs = [dev(z=(z + r) % 4) for r in (1, 2, 3)]

    pending = []

    def copy(src, dst, send, recv, to):
        return pltpu.make_async_remote_copy(
            src_ref=src, dst_ref=dst, send_sem=send, recv_sem=recv, device_id=to, device_id_type=MESH
        )

    def start(cp):
        cp.start()
        pending.append(cp)

    def send(src, dst, i, to):
        start(copy(src, dst, ss.at[i], rs.at[i], to))

    def pass_on(ref, i, to):
        send(ref, ref, i, to)

    def got(dst, i):
        copy(dst, dst, ss.at[i], rs.at[i], d_c).wait_recv()

    def span(i, n):
        return pl.ds(pl.multiple_of(i * n, n), n)

    s_o = hi * 2 + z0
    s_y = (1 - hi) * 2 + z0
    s_z = hi * 2 + 1 - z0
    s_d = (1 - hi) * 2 + 1 - z0
    here, there = hi * 2 + c, (1 - hi) * 2 + c
    here_c, there_c = hi * 2 + 1 - c, (1 - hi) * 2 + 1 - c
    own_k, other_k = pl.ds(0, kg), pl.ds(kg, kg)

    def h_at(i, k):
        return hbuf.at[span(i, depth), k]

    l_a = [pltpu.make_async_copy(a.at[pl.ds(k * qr, qr)], abuf.at[s_o, k, c], loc.at[k]) for k in range(4)]
    l_b = pltpu.make_async_copy(b, bbuf.at[:, pl.ds(0, kb)], loc.at[4])
    l_g = pltpu.make_async_copy(g.at[span(c * 2 + hi, rows // 2)], gbuf.at[x, :, span(here, depth)], loc.at[5])
    l_h = pltpu.make_async_copy(h, h_at(here, own_k), loc.at[6])
    for cp in (*l_a, l_b, l_g, l_h):
        cp.start()

    barrier = pltpu.get_barrier_semaphore()
    friends = [d_y, d_c, d_yc, d_l, d_b] + d_x + d_zs
    for to in friends:
        pl.semaphore_signal(barrier, inc=1, device_id=to, device_id_type=MESH)
    pl.semaphore_wait(barrier, len(friends))

    def send_g(i, hh, cc, to):
        send(g.at[span(cc * 2 + hh, rows // 2)], gbuf.at[x, :, span(here, depth)], i, to)

    def send_a(k, i, to):
        send(a.at[pl.ds(k * qr, qr)], abuf.at[s_o, k, c], i, to)

    def b_at(piece):
        return bbuf.at[:, pl.ds(kb + piece[1], piece[2])]

    def send_b(piece, i):
        send(b.at[:, pl.ds(piece[1], piece[2])], b_at(piece), i, d_q)

    send_g(0, 1 - hi, c, d_y)
    send_g(1, 1 - hi, 1 - c, d_yc)
    send_a(0, 2, d_y)
    send_a(2, 3, d_z)
    send_b(FIRST, 4)
    send_a(1, 5, d_y)
    send_a(3, 6, d_z)
    for k in range(4):
        send_a(k, 7 + k, d_c)
    send_g(11, hi, 1 - c, d_c)
    send(h, h_at(here, own_k), 14, d_c)
    send_a(2, 15, d_y)
    send_a(0, 16, d_z)
    send_a(3, 17, d_y)
    send_a(1, 18, d_z)
    send(h, h_at(here, other_k), 12, d_l)
    send(h, h_at(here, other_k), 13, d_b)
    send_b(REST, 19)

    def x_copy(s, q, ch, r):
        pb, c0, w = PIECES[ch]
        u, qs, cs = s * 4 + q[0], pl.ds(*q), pl.ds(c0, w)
        return copy(
            stg.at[s, qs, pb, span((x + r) % 4, xrows), cs], rx.at[r - 1, s, qs, pb, :, cs],
            xs.at[u, ch, r - 1], xr.at[u, ch, r - 1], d_x[r - 1],
        )

    def block(s, q, *chunks):
        qs = pl.ds(*q)
        c0 = PIECES[chunks[0]][0] * kb + PIECES[chunks[0]][1]
        w = sum(PIECES[ch][2] for ch in chunks)
        lhs = abuf[s, qs].reshape(q[1] * 2 * qr, feats)
        part = jnp.dot(lhs, bbuf[:, pl.ds(c0, w)], preferred_element_type=F32)
        for ch in chunks:
            pb, first, width = PIECES[ch]
            cut = part[:, pb * kb + first - c0:][:, :width].reshape(q[1], 2 * qr, width)
            cf[pl.ds(0, q[1]), pb, :, pl.ds(first, width)] = cut
            stg[s, qs, pb, :, pl.ds(first, width)] = cut.astype(BF)
        for ch in chunks:
            for m in MESSAGES[q]:
                for r in (1, 2, 3):
                    x_copy(s, m, ch, r).start()
        for ch in chunks:
            pb, first, width = PIECES[ch]
            cs = pl.ds(first, width)
            acc[s, qs, pb, :, cs] = cf[pl.ds(0, q[1]), pb, span(x, xrows), cs]

    def span_of(chunks):
        return PIECES[chunks[0]][0], pl.ds(PIECES[chunks[0]][1], sum(PIECES[ch][2] for ch in chunks))

    def add_x(i, zz, q, *chunks):
        qs = pl.ds(*q)
        pb, cs = span_of(chunks)
        for hh in (1 - lo, lo):
            s = hh * 2 + zz
            for m in MESSAGES[q]:
                for ch in chunks:
                    for r in range(3):
                        ref = rx.at[r, s, pl.ds(*m), pb, :, pl.ds(*PIECES[ch][1:])]
                        copy(ref, ref, xs.at[0, 0, 0], xr.at[s * 4 + m[0], ch, r], d_c).wait_recv()
            total = acc[s, qs, pb, :, cs]
            for r in range(3):
                total = total + rx[r, s, qs, pb, :, cs].astype(F32)
            if hh is lo:
                acc[s, qs, pb, :, cs] = total
            else:
                ref = lst.at[zz, qs, pb, :, cs]
                ref[...] = total.astype(lst.dtype)
                start(copy(ref, lrx.at[zz, qs, pb, :, cs], ls.at[i], lr.at[i], d_l))

    def add_y(i, zz, q, *chunks):
        qs = pl.ds(*q)
        pb, cs = span_of(chunks)
        ref = lrx.at[zz, qs, pb, :, cs]
        copy(ref, ref, ls.at[i], lr.at[i], d_c).wait_recv()
        pin[pb, zz, qs, x, :, cs] = (acc[lo * 2 + zz, qs, pb, :, cs] + lrx[zz, qs, pb, :, cs].astype(F32)).astype(BF)
        for r in (1, 2, 3):
            ref = pin.at[pb, zz, qs, x, :, cs]
            start(copy(ref, ref, ps.at[i, r - 1], pr.at[i, r - 1], d_x[r - 1]))

    def gathered(i, zz, q, *chunks):
        pb, cs = span_of(chunks)
        for r in (1, 2, 3):
            ref = pin.at[pb, zz, pl.ds(*q), (x + 4 - r) % 4, :, cs]
            copy(ref, ref, ps.at[i, r - 1], pr.at[i, r - 1], d_c).wait_recv()

    for cp in l_a:
        cp.wait()
    l_b.wait()
    for k in range(4):
        got(abuf.at[s_o, k, 1 - c], 7 + k)
    block(s_o, TOP, 0)
    block(s_o, LOW, 0)

    l_g.wait()
    got(gbuf.at[x, :, span(here_c, depth)], 11)
    got(gbuf.at[x, :, span(there, depth)], 0)
    got(gbuf.at[x, :, span(there_c, depth)], 1)
    for r in (1, 2, 3):
        start(copy(gbuf.at[x], gbuf.at[x], gs.at[r - 1], gr.at[r - 1], d_x[r - 1]))

    got(abuf.at[s_z, 2, c], 3)
    pass_on(abuf.at[s_z, 2, c], 20, d_c)
    got(abuf.at[s_z, 3, c], 6)
    pass_on(abuf.at[s_z, 3, c], 21, d_c)
    got(abuf.at[s_y, 0, c], 2)
    pass_on(abuf.at[s_y, 0, c], 22, d_c)
    got(abuf.at[s_z, 2, 1 - c], 20)
    got(abuf.at[s_z, 3, 1 - c], 21)
    block(s_z, LOW, 0)
    got(abuf.at[s_y, 1, c], 5)
    pass_on(abuf.at[s_y, 1, c], 23, d_c)
    got(abuf.at[s_y, 0, 1 - c], 22)
    got(abuf.at[s_y, 1, 1 - c], 23)
    block(s_y, TOP, 0)

    got(abuf.at[s_z, 0, c], 16)
    pass_on(abuf.at[s_y, 0, c], 28, d_z)
    pass_on(abuf.at[s_z, 0, c], 29, d_c)
    got(b_at(FIRST), 4)
    got(abuf.at[s_z, 1, c], 18)
    pass_on(abuf.at[s_y, 1, c], 30, d_z)
    pass_on(abuf.at[s_z, 1, c], 31, d_c)
    block(s_o, TOP, 1)
    block(s_y, TOP, 1)
    got(abuf.at[s_z, 0, 1 - c], 29)
    got(abuf.at[s_z, 1, 1 - c], 31)
    block(s_z, TOP, 0)
    block(s_o, LOW, 1)
    got(abuf.at[s_y, 2, c], 15)
    pass_on(abuf.at[s_y, 2, c], 33, d_c)

    third_z = copy(abuf.at[s_y, 2, c], abuf.at[s_y, 2, c], ss.at[32], rs.at[32], d_z)
    third_y = copy(abuf.at[s_z, 2, c], abuf.at[s_z, 2, c], ss.at[32], rs.at[32], d_y)
    pending.append(third_z)

    @pl.when(c == 0)
    def _():
        third_z.start()

    add_x(0, z0, TOP, 0)
    add_x(1, z0, TOP, 1)
    got(abuf.at[s_y, 3, c], 17)
    pass_on(abuf.at[s_y, 3, c], 35, d_c)
    block(s_z, TOP, 1)
    got(abuf.at[s_y, 2, 1 - c], 33)
    got(abuf.at[s_y, 3, 1 - c], 35)
    block(s_y, LOW, 0, 1)
    block(s_z, LOW, 1)

    h2 = depth // 2
    got(h_at(here, other_k), 12)
    send(hbuf.at[span(here * 2, h2), other_k], hbuf.at[span(here * 2, h2), own_k], 24, d_b)
    got(h_at(there, other_k), 13)
    send(hbuf.at[span(there * 2 + 1, h2), other_k], hbuf.at[span(there * 2 + 1, h2), own_k], 26, d_l)
    pass_on(h_at(here, other_k), 25, d_c)
    pass_on(h_at(there, other_k), 27, d_c)
    add_x(2, z0, LOW, 0)
    add_x(3, z0, LOW, 1)
    pass_on(abuf.at[s_z, 3, c], 34, d_y)
    add_y(0, z0, TOP, 0)
    add_y(1, z0, TOP, 1)

    got(hbuf.at[span(there * 2, h2), own_k], 24)
    got(hbuf.at[span(there * 2 + 1, h2), own_k], 26)
    pass_on(h_at(there, own_k), 36, d_c)
    l_h.wait()
    got(h_at(here_c, own_k), 14)
    got(h_at(here_c, other_k), 25)
    got(h_at(there_c, other_k), 27)
    for r in (1, 2, 3):
        src = (x + 4 - r) % 4
        copy(gbuf.at[src], gbuf.at[src], gs.at[r - 1], gr.at[r - 1], d_c).wait_recv()
    got(h_at(there_c, own_k), 36)
    part = jnp.dot(gbuf[...].reshape(2 * rows, 4 * depth), hbuf[...], preferred_element_type=F32)
    for k in (0, 1):
        cut = part[:, k * kg:][:, :kg].reshape(4, rows // 2, kg)
        zall[:, k] = cut
        zst[:, k] = cut.astype(zst.dtype)
    for r in (1, 2, 3):
        start(copy(zst.at[(z + r) % 4], zrx.at[r - 1], zs.at[r - 1], zr.at[r - 1], d_zs[r - 1]))
    add_y(2, z0, LOW, 0)
    add_y(3, z0, LOW, 1)

    got(b_at(REST), 19)

    @pl.loop(0, 3)
    def _(j):
        s = jnp.where(j == 0, s_o, jnp.where(j == 1, s_z, s_y))
        block(s, TOP, 2)
        block(s, LOW, 2)

    got(abuf.at[s_d, 0, c], 28)
    pass_on(abuf.at[s_d, 0, c], 37, d_c)
    got(abuf.at[s_d, 1, c], 30)
    pass_on(abuf.at[s_d, 1, c], 38, d_c)

    @pl.when(c == 1)
    def _():
        third_y.start()

    got(abuf.at[s_d, 0, 1 - c], 37)
    got(abuf.at[s_d, 1, 1 - c], 38)
    block(s_d, TOP, 0, 1, 2)
    add_x(4, z0, ALL, 2)

    mine, theirs = span(hi, 2), span(1 - hi, 2)
    for r in (1, 2, 3):
        copy(zst.at[0], zrx.at[r - 1], zs.at[r - 1], zr.at[r - 1], d_c).wait_recv()
    for k in (0, 1):
        total = zall[z, k] + zrx[0, k].astype(F32) + zrx[1, k].astype(F32) + zrx[2, k].astype(F32)
        pout[k, z0, mine, c] = total.astype(BF).reshape(2, qr, kg)
    pass_on(pout.at[:, z0, mine, c], 41, d_y)
    pass_on(pout.at[:, z0, mine, c], 45, d_z)
    pass_on(pout.at[:, z0, mine, c], 43, d_c)

    got(abuf.at[s_d, 3, c], 34)
    pass_on(abuf.at[s_d, 3, c], 40, d_c)
    got(abuf.at[s_d, 2, c], 32)
    pass_on(abuf.at[s_d, 2, c], 39, d_c)
    got(abuf.at[s_d, 3, 1 - c], 40)
    block(s_d, FOURTH, 0, 1, 2)
    add_x(5, 1 - z0, TOP, 1, 2)
    add_x(6, 1 - z0, TOP, 0)
    got(abuf.at[s_d, 2, 1 - c], 39)
    block(s_d, THIRD, 0, 1, 2)

    add_y(4, z0, ALL, 2)
    got(pout.at[:, z0, theirs, c], 41)
    pass_on(pout.at[:, z0, theirs, c], 42, d_z)
    pass_on(pout.at[:, z0, theirs, c], 46, d_c)
    add_y(5, 1 - z0, TOP, 1, 2)
    add_y(6, 1 - z0, TOP, 0)
    got(pout.at[:, 1 - z0, mine, c], 45)
    pass_on(pout.at[:, 1 - z0, mine, c], 44, d_c)
    add_x(7, 1 - z0, LOW, 1, 2)
    add_x(8, 1 - z0, LOW, 0)
    got(pout.at[:, 1 - z0, theirs, c], 42)
    pass_on(pout.at[:, 1 - z0, theirs, c], 47, d_c)
    add_y(7, 1 - z0, LOW, 1, 2)
    add_y(8, 1 - z0, LOW, 0)

    got(pout.at[:, z0, mine, 1 - c], 43)
    got(pout.at[:, z0, theirs, 1 - c], 46)
    got(pout.at[:, 1 - z0, mine, 1 - c], 44)
    got(pout.at[:, 1 - z0, theirs, 1 - c], 47)

    def squares(k, pb):
        left = pout[k].reshape(4 * rows, kg)
        right = pin[pb].reshape(4 * rows, kb)
        t = lax.dot_general(left, right, (((0,), (0,)), ((), ())), preferred_element_type=F32)
        return t * t

    hk = kg // 2
    upper, lower = pl.ds(0, hk), pl.ds(hk, hk)

    def e_copy(i, to):
        return copy(est.at[i], erx.at[i], es.at[i], er.at[i], to)

    def give(i, values, to):
        est[i] = values.astype(est.dtype)
        start(e_copy(i, to))

    def taken(i):
        e_copy(i, d_c).wait_recv()
        return erx[i].astype(F32)

    gathered(1, z0, TOP, 1)
    gathered(3, z0, LOW, 1)
    gathered(4, z0, ALL, 2)
    gathered(5, 1 - z0, TOP, 1, 2)
    gathered(7, 1 - z0, LOW, 1, 2)
    quad = squares(1, 1)
    give(0, quad[:hk], d_l)
    give(1, quad[hk:], d_q)
    quad = squares(0, 1)
    esum[0] = quad[:hk]
    give(2, quad[hk:], d_q)
    gathered(0, z0, TOP, 0)
    gathered(2, z0, LOW, 0)
    gathered(6, 1 - z0, TOP, 0)
    gathered(8, 1 - z0, LOW, 0)
    quad = squares(1, 0)
    esum[1] = quad[hk:]
    give(3, quad[:hk], d_l)
    give(4, esum[0] + taken(0), d_q)
    give(5, esum[1] + taken(1), d_l)
    total = squares(0, 0)
    out[lower] = total[hk:]
    out[upper] = total[:hk] + taken(3)
    out[lower] = out[lower] + taken(2)
    out[upper] = (out[upper] + taken(4)) * 0.25
    out[lower] = (out[lower] + taken(5)) * 0.25

    for cp in pending:
        cp.wait_send()

    @pl.loop(0, 4)
    def _(s):
        for m in (TOP, THIRD, FOURTH):
            for ch in range(3):
                for r in (1, 2, 3):
                    x_copy(s, m, ch, r).wait_send()


def per_device(acts, grads, basis_in, basis_out):
    rows, feats = acts.shape
    kb = basis_in.shape[1]
    depth, kg = basis_out.shape
    dma = pltpu.SemaphoreType.DMA
    return pl.pallas_call(
        kernel,
        out_shape=jax.ShapeDtypeStruct((kg, kb), F32),
        in_specs=[pl.BlockSpec(memory_space=pl.ANY)] * 4,
        out_specs=pl.BlockSpec(memory_space=pltpu.VMEM),
        scratch_shapes=[
            pltpu.VMEM((4, 4, 2, rows // 4, feats), BF),
            pltpu.VMEM((feats, 2 * kb), BF),
            pltpu.VMEM((4, rows // 2, 4 * depth), BF),
            pltpu.VMEM((4 * depth, 2 * kg), BF),
            pltpu.VMEM((2, 2, rows // 2, kb), F32),
            pltpu.VMEM((4, 4, 2, rows // 2, kb), BF),
            pltpu.VMEM((4, 4, 2, rows // 8, kb), F32),
            pltpu.VMEM((3, 4, 4, 2, rows // 8, kb), BF),
            pltpu.VMEM((2, 4, 2, rows // 8, kb), BF),
            pltpu.VMEM((2, 4, 2, rows // 8, kb), BF),
            pltpu.VMEM((2, 2, 4, 4, rows // 8, kb), BF),
            pltpu.VMEM((4, 2, rows // 2, kg), BF),
            pltpu.VMEM((4, 2, rows // 2, kg), F32),
            pltpu.VMEM((3, 2, rows // 2, kg), BF),
            pltpu.VMEM((2, 2, 4, 2, rows // 4, kg), BF),
            pltpu.VMEM((6, kg // 2, kb), BF),
            pltpu.VMEM((6, kg // 2, kb), BF),
            pltpu.VMEM((2, kg // 2, kb), F32),
            dma((7,)),
            dma((48,)), dma((48,)),
            dma((16, 3, 3)), dma((16, 3, 3)),
            dma((9,)), dma((9,)),
            dma((9, 3)), dma((9, 3)),
            dma((3,)), dma((3,)),
            dma((3,)), dma((3,)),
            dma((6,)), dma((6,)),
        ],
        compiler_params=pltpu.CompilerParams(
            collective_id=0, has_side_effects=True, vmem_limit_bytes=58 * 2**20
        ),
        cost_estimate=pl.CostEstimate(flops=14 * 10**9, bytes_accessed=7 * 10**6, transcendentals=0),
    )(acts, basis_in, grads, basis_out)


def solution(mesh):
    in_specs = (P("col", "row"), P("row", "col"), P("row", "col"), P("col", "row"))
    return jax.shard_map(
        per_device, mesh=mesh, in_specs=in_specs, out_specs=P("row", "col"), check_vma=False
    )
```

```python
import jax
import jax.numpy as jnp
from jax import lax
from jax.experimental import pallas as pl
from jax.experimental.pallas import tpu as pltpu
from jax.sharding import PartitionSpec as P

BF = jnp.bfloat16
F32 = jnp.float32
MESH = pl.DeviceIdType.MESH
OWN, FIRST, REST = (0, 0, 384), (1, 0, 256), (1, 256, 128)
PIECES = (OWN, FIRST, REST)
TOP, LOW, THIRD, FOURTH, ALL = (0, 2), (2, 2), (2, 1), (3, 1), (0, 4)
MESSAGES = {TOP: [TOP], LOW: [THIRD, FOURTH], THIRD: [THIRD], FOURTH: [FOURTH], ALL: [TOP, THIRD, FOURTH]}
NEAR = {(0, 0): 0, (0, 1): 1, (0, 2): 4, (2, 0): 2, (2, 1): 3, (2, 2): 4}
FAR = {(0, 0): 6, (0, 1): 5, (0, 2): 5, (2, 0): 8, (2, 1): 7, (2, 2): 7}


def kernel(
    a, b, g, h, out,
    abuf, bbuf, gbuf, hbuf,
    cf, stg, acc, rx, lst, lrx, pin,
    zst, zall, zrx, pout,
    est, erx, esum,
    loc, ss, rs, xs, xr, ls, lr, ps, pr, gs, gr, zs, zr, es, er,
):
    row, col = lax.axis_index("row"), lax.axis_index("col")
    lo, x = row // 4, row % 4
    c, z, hi = col % 2, (col // 2) % 4, col // 8
    z0 = z % 2
    rows, feats = a.shape
    qr = rows // 4
    xrows = 2 * qr // 4
    depth, kg = h.shape
    kb = b.shape[1]

    def dev(x=x, lo=lo, hi=hi, z=z, c=c):
        return (lo * 4 + x, (hi * 4 + z) * 2 + c)

    d_y = dev(hi=1 - hi)
    d_z = dev(z=z + 1 - 2 * z0)
    d_q = dev(z=3 - z)
    d_c = dev(c=1 - c)
    d_yc = dev(hi=1 - hi, c=1 - c)
    d_l = dev(lo=1 - lo)
    d_b = dev(lo=1 - lo, hi=1 - hi)
    d_x = [dev(x=(x + r) % 4) for r in (1, 2, 3)]
    d_zs = [dev(z=(z + r) % 4) for r in (1, 2, 3)]

    pending = []

    def copy(src, dst, send, recv, to):
        return pltpu.make_async_remote_copy(
            src_ref=src, dst_ref=dst, send_sem=send, recv_sem=recv, device_id=to, device_id_type=MESH
        )

    def start(cp):
        cp.start()
        pending.append(cp)

    def send(src, dst, i, to):
        start(copy(src, dst, ss.at[i], rs.at[i], to))

    def pass_on(ref, i, to):
        send(ref, ref, i, to)

    def got(dst, i):
        copy(dst, dst, ss.at[i], rs.at[i], d_c).wait_recv()

    def span(i, n):
        return pl.ds(pl.multiple_of(i * n, n), n)

    s_o = hi * 2 + z0
    s_y = (1 - hi) * 2 + z0
    s_z = hi * 2 + 1 - z0
    s_d = (1 - hi) * 2 + 1 - z0
    here, there = hi * 2 + c, (1 - hi) * 2 + c
    here_c, there_c = hi * 2 + 1 - c, (1 - hi) * 2 + 1 - c
    own_k, other_k = pl.ds(0, kg), pl.ds(kg, kg)

    def h_at(i, k):
        return hbuf.at[span(i, depth), k]

    l_a = [pltpu.make_async_copy(a.at[pl.ds(k * qr, qr)], abuf.at[s_o, k, c], loc.at[k]) for k in range(4)]
    l_b = pltpu.make_async_copy(b, bbuf.at[:, pl.ds(0, kb)], loc.at[4])
    l_g = pltpu.make_async_copy(g.at[span(c * 2 + hi, rows // 2)], gbuf.at[x, :, span(here, depth)], loc.at[5])
    l_h = pltpu.make_async_copy(h, h_at(here, own_k), loc.at[6])
    for cp in (*l_a, l_b, l_g, l_h):
        cp.start()

    barrier = pltpu.get_barrier_semaphore()
    friends = [d_y, d_c, d_yc, d_l, d_b] + d_x + d_zs
    for to in friends:
        pl.semaphore_signal(barrier, inc=1, device_id=to, device_id_type=MESH)
    pl.semaphore_wait(barrier, len(friends))

    def send_g(i, hh, cc, to):
        send(g.at[span(cc * 2 + hh, rows // 2)], gbuf.at[x, :, span(here, depth)], i, to)

    def send_a(k, i, to):
        send(a.at[pl.ds(k * qr, qr)], abuf.at[s_o, k, c], i, to)

    def b_at(piece):
        return bbuf.at[:, pl.ds(kb + piece[1], piece[2])]

    def send_b(piece, i):
        send(b.at[:, pl.ds(piece[1], piece[2])], b_at(piece), i, d_q)

    send_g(0, 1 - hi, c, d_y)
    send_g(1, 1 - hi, 1 - c, d_yc)
    send_a(0, 2, d_y)
    send_a(2, 3, d_z)
    send_b(FIRST, 4)
    send_a(1, 5, d_y)
    send_a(3, 6, d_z)
    for k in range(4):
        send_a(k, 7 + k, d_c)
    send_g(11, hi, 1 - c, d_c)
    send(h, h_at(here, own_k), 14, d_c)
    send_a(2, 15, d_y)
    send_a(0, 16, d_z)
    send_a(3, 17, d_y)
    send_a(1, 18, d_z)
    send(h, h_at(here, other_k), 12, d_l)
    send(h, h_at(here, other_k), 13, d_b)
    send_b(REST, 19)

    def x_copy(s, q, ch, r):
        pb, c0, w = PIECES[ch]
        qs, cs = pl.ds(*q), pl.ds(c0, w)
        key = (0 if q[0] == 0 else 2, ch)
        piece = jnp.where(s % 2 == z0, NEAR[key], FAR[key])
        return copy(
            stg.at[s, qs, pb, span((x + r) % 4, xrows), cs], rx.at[r - 1, s, qs, pb, :, cs],
            xs.at[0], xr.at[piece, s // 2], d_x[r - 1],
        )

    def block(s, q, *chunks):
        qs = pl.ds(*q)
        c0 = PIECES[chunks[0]][0] * kb + PIECES[chunks[0]][1]
        w = sum(PIECES[ch][2] for ch in chunks)
        lhs = abuf[s, qs].reshape(q[1] * 2 * qr, feats)
        part = jnp.dot(lhs, bbuf[:, pl.ds(c0, w)], preferred_element_type=F32)
        for ch in chunks:
            pb, first, width = PIECES[ch]
            cut = part[:, pb * kb + first - c0:][:, :width].reshape(q[1], 2 * qr, width)
            cf[pl.ds(0, q[1]), pb, :, pl.ds(first, width)] = cut
            stg[s, qs, pb, :, pl.ds(first, width)] = cut.astype(BF)
        for ch in chunks:
            for m in MESSAGES[q]:
                for r in (1, 2, 3):
                    x_copy(s, m, ch, r).start()
        for ch in chunks:
            pb, first, width = PIECES[ch]
            cs = pl.ds(first, width)
            acc[s, qs, pb, :, cs] = cf[pl.ds(0, q[1]), pb, span(x, xrows), cs]

    def span_of(chunks):
        return PIECES[chunks[0]][0], pl.ds(PIECES[chunks[0]][1], sum(PIECES[ch][2] for ch in chunks))

    def add_x(i, zz, q, *chunks):
        qs = pl.ds(*q)
        pb, cs = span_of(chunks)
        for hh in (1 - lo, lo):
            s = hh * 2 + zz
            ref = rx.at[:, s, qs, pb, :, cs]
            copy(ref, ref, xs.at[0], xr.at[i, hh], d_c).wait_recv()
            total = acc[s, qs, pb, :, cs]
            for r in range(3):
                total = total + rx[r, s, qs, pb, :, cs].astype(F32)
            if hh is lo:
                acc[s, qs, pb, :, cs] = total
            else:
                ref = lst.at[zz, qs, pb, :, cs]
                ref[...] = total.astype(lst.dtype)
                copy(ref, lrx.at[zz, qs, pb, :, cs], ls.at[0], lr.at[i], d_l).start()

    def add_y(i, zz, q, *chunks):
        qs = pl.ds(*q)
        pb, cs = span_of(chunks)
        ref = lrx.at[zz, qs, pb, :, cs]
        copy(ref, ref, ls.at[0], lr.at[i], d_c).wait_recv()
        pin[pb, zz, qs, x, :, cs] = (acc[lo * 2 + zz, qs, pb, :, cs] + lrx[zz, qs, pb, :, cs].astype(F32)).astype(BF)
        for r in (1, 2, 3):
            ref = pin.at[pb, zz, qs, x, :, cs]
            copy(ref, ref, ps.at[0], pr.at[i], d_x[r - 1]).start()

    def gathered(i, zz, q, *chunks):
        pb, cs = span_of(chunks)
        ref = pin.at[pb, zz, pl.ds(*q), pl.ds(0, 3), :, cs]
        copy(ref, ref, ps.at[0], pr.at[i], d_c).wait_recv()

    for cp in l_a:
        cp.wait()
    l_b.wait()
    for k in range(4):
        got(abuf.at[s_o, k, 1 - c], 7 + k)
    block(s_o, TOP, 0)
    block(s_o, LOW, 0)

    l_g.wait()
    got(gbuf.at[x, :, span(here_c, depth)], 11)
    got(gbuf.at[x, :, span(there, depth)], 0)
    got(gbuf.at[x, :, span(there_c, depth)], 1)
    for r in (1, 2, 3):
        start(copy(gbuf.at[x], gbuf.at[x], gs.at[r - 1], gr.at[r - 1], d_x[r - 1]))

    got(abuf.at[s_z, 2, c], 3)
    pass_on(abuf.at[s_z, 2, c], 20, d_c)
    got(abuf.at[s_z, 3, c], 6)
    pass_on(abuf.at[s_z, 3, c], 21, d_c)
    got(abuf.at[s_y, 0, c], 2)
    pass_on(abuf.at[s_y, 0, c], 22, d_c)
    got(abuf.at[s_z, 2, 1 - c], 20)
    got(abuf.at[s_z, 3, 1 - c], 21)
    block(s_z, LOW, 0)
    got(abuf.at[s_y, 1, c], 5)
    pass_on(abuf.at[s_y, 1, c], 23, d_c)
    got(abuf.at[s_y, 0, 1 - c], 22)
    got(abuf.at[s_y, 1, 1 - c], 23)
    block(s_y, TOP, 0)

    got(abuf.at[s_z, 0, c], 16)
    pass_on(abuf.at[s_y, 0, c], 28, d_z)
    pass_on(abuf.at[s_z, 0, c], 29, d_c)
    got(b_at(FIRST), 4)
    got(abuf.at[s_z, 1, c], 18)
    pass_on(abuf.at[s_y, 1, c], 30, d_z)
    pass_on(abuf.at[s_z, 1, c], 31, d_c)
    block(s_o, TOP, 1)
    block(s_y, TOP, 1)
    got(abuf.at[s_z, 0, 1 - c], 29)
    got(abuf.at[s_z, 1, 1 - c], 31)
    block(s_z, TOP, 0)
    block(s_o, LOW, 1)
    got(abuf.at[s_y, 2, c], 15)
    pass_on(abuf.at[s_y, 2, c], 33, d_c)

    third_z = copy(abuf.at[s_y, 2, c], abuf.at[s_y, 2, c], ss.at[32], rs.at[32], d_z)
    third_y = copy(abuf.at[s_z, 2, c], abuf.at[s_z, 2, c], ss.at[32], rs.at[32], d_y)
    pending.append(third_z)

    @pl.when(c == 0)
    def _():
        third_z.start()

    add_x(0, z0, TOP, 0)
    add_x(1, z0, TOP, 1)
    got(abuf.at[s_y, 3, c], 17)
    pass_on(abuf.at[s_y, 3, c], 35, d_c)
    block(s_z, TOP, 1)
    got(abuf.at[s_y, 2, 1 - c], 33)
    got(abuf.at[s_y, 3, 1 - c], 35)
    block(s_y, LOW, 0, 1)
    block(s_z, LOW, 1)

    h2 = depth // 2
    got(h_at(here, other_k), 12)
    send(hbuf.at[span(here * 2, h2), other_k], hbuf.at[span(here * 2, h2), own_k], 24, d_b)
    got(h_at(there, other_k), 13)
    send(hbuf.at[span(there * 2 + 1, h2), other_k], hbuf.at[span(there * 2 + 1, h2), own_k], 26, d_l)
    pass_on(h_at(here, other_k), 25, d_c)
    pass_on(h_at(there, other_k), 27, d_c)
    add_x(2, z0, LOW, 0)
    add_x(3, z0, LOW, 1)
    pass_on(abuf.at[s_z, 3, c], 34, d_y)
    add_y(0, z0, TOP, 0)
    add_y(1, z0, TOP, 1)

    got(hbuf.at[span(there * 2, h2), own_k], 24)
    got(hbuf.at[span(there * 2 + 1, h2), own_k], 26)
    pass_on(h_at(there, own_k), 36, d_c)
    l_h.wait()
    got(h_at(here_c, own_k), 14)
    got(h_at(here_c, other_k), 25)
    got(h_at(there_c, other_k), 27)
    for r in (1, 2, 3):
        src = (x + 4 - r) % 4
        copy(gbuf.at[src], gbuf.at[src], gs.at[r - 1], gr.at[r - 1], d_c).wait_recv()
    got(h_at(there_c, own_k), 36)
    part = jnp.dot(gbuf[...].reshape(2 * rows, 4 * depth), hbuf[...], preferred_element_type=F32)
    for k in (0, 1):
        cut = part[:, k * kg:][:, :kg].reshape(4, rows // 2, kg)
        zall[:, k] = cut
        zst[:, k] = cut.astype(zst.dtype)
    for r in (1, 2, 3):
        start(copy(zst.at[(z + r) % 4], zrx.at[r - 1], zs.at[r - 1], zr.at[r - 1], d_zs[r - 1]))
    add_y(2, z0, LOW, 0)
    add_y(3, z0, LOW, 1)

    got(b_at(REST), 19)

    @pl.loop(0, 3)
    def _(j):
        s = jnp.where(j == 0, s_o, jnp.where(j == 1, s_z, s_y))
        block(s, TOP, 2)
        block(s, LOW, 2)

    got(abuf.at[s_d, 0, c], 28)
    pass_on(abuf.at[s_d, 0, c], 37, d_c)
    got(abuf.at[s_d, 1, c], 30)
    pass_on(abuf.at[s_d, 1, c], 38, d_c)

    @pl.when(c == 1)
    def _():
        third_y.start()

    got(abuf.at[s_d, 0, 1 - c], 37)
    got(abuf.at[s_d, 1, 1 - c], 38)
    block(s_d, TOP, 0, 1, 2)
    add_x(4, z0, ALL, 2)

    mine, theirs = span(hi, 2), span(1 - hi, 2)
    for r in (1, 2, 3):
        copy(zst.at[0], zrx.at[r - 1], zs.at[r - 1], zr.at[r - 1], d_c).wait_recv()
    for k in (0, 1):
        total = zall[z, k] + zrx[0, k].astype(F32) + zrx[1, k].astype(F32) + zrx[2, k].astype(F32)
        pout[k, z0, mine, c] = total.astype(BF).reshape(2, qr, kg)
    pass_on(pout.at[:, z0, mine, c], 41, d_y)
    pass_on(pout.at[:, z0, mine, c], 45, d_z)
    pass_on(pout.at[:, z0, mine, c], 43, d_c)

    got(abuf.at[s_d, 3, c], 34)
    pass_on(abuf.at[s_d, 3, c], 40, d_c)
    got(abuf.at[s_d, 2, c], 32)
    pass_on(abuf.at[s_d, 2, c], 39, d_c)
    got(abuf.at[s_d, 3, 1 - c], 40)
    block(s_d, FOURTH, 0, 1, 2)
    add_x(5, 1 - z0, TOP, 1, 2)
    add_x(6, 1 - z0, TOP, 0)
    got(abuf.at[s_d, 2, 1 - c], 39)
    block(s_d, THIRD, 0, 1, 2)

    add_y(4, z0, ALL, 2)
    got(pout.at[:, z0, theirs, c], 41)
    pass_on(pout.at[:, z0, theirs, c], 42, d_z)
    pass_on(pout.at[:, z0, theirs, c], 46, d_c)
    add_y(5, 1 - z0, TOP, 1, 2)
    add_y(6, 1 - z0, TOP, 0)
    got(pout.at[:, 1 - z0, mine, c], 45)
    pass_on(pout.at[:, 1 - z0, mine, c], 44, d_c)
    add_x(7, 1 - z0, LOW, 1, 2)
    add_x(8, 1 - z0, LOW, 0)
    got(pout.at[:, 1 - z0, theirs, c], 42)
    pass_on(pout.at[:, 1 - z0, theirs, c], 47, d_c)
    add_y(7, 1 - z0, LOW, 1, 2)
    add_y(8, 1 - z0, LOW, 0)

    got(pout.at[:, z0, mine, 1 - c], 43)
    got(pout.at[:, z0, theirs, 1 - c], 46)
    got(pout.at[:, 1 - z0, mine, 1 - c], 44)
    got(pout.at[:, 1 - z0, theirs, 1 - c], 47)

    def squares(k, pb):
        left = pout[k].reshape(4 * rows, kg)
        right = pin[pb].reshape(4 * rows, kb)
        t = lax.dot_general(left, right, (((0,), (0,)), ((), ())), preferred_element_type=F32)
        return t * t

    hk = kg // 2
    upper, lower = pl.ds(0, hk), pl.ds(hk, hk)

    def e_copy(i, to):
        return copy(est.at[i], erx.at[i], es.at[i], er.at[i], to)

    def give(i, values, to):
        est[i] = values.astype(est.dtype)
        start(e_copy(i, to))

    def taken(i):
        e_copy(i, d_c).wait_recv()
        return erx[i].astype(F32)

    gathered(1, z0, TOP, 1)
    gathered(3, z0, LOW, 1)
    gathered(4, z0, ALL, 2)
    gathered(5, 1 - z0, TOP, 1, 2)
    gathered(7, 1 - z0, LOW, 1, 2)
    quad = squares(1, 1)
    give(0, quad[:hk], d_l)
    give(1, quad[hk:], d_q)
    quad = squares(0, 1)
    esum[0] = quad[:hk]
    give(2, quad[hk:], d_q)
    gathered(0, z0, TOP, 0)
    gathered(2, z0, LOW, 0)
    gathered(6, 1 - z0, TOP, 0)
    gathered(8, 1 - z0, LOW, 0)
    quad = squares(1, 0)
    esum[1] = quad[hk:]
    give(3, quad[:hk], d_l)
    give(4, esum[0] + taken(0), d_q)
    give(5, esum[1] + taken(1), d_l)
    total = squares(0, 0)
    out[lower] = total[hk:]
    out[upper] = total[:hk] + taken(3)
    out[lower] = out[lower] + taken(2)
    out[upper] = (out[upper] + taken(4)) * 0.25
    out[lower] = (out[lower] + taken(5)) * 0.25

    for cp in pending:
        cp.wait_send()

    for ref, sem in ((stg.at[:, :, :, pl.ds(0, 3 * xrows)], xs), (lst, ls), (pin.at[:, :, :, pl.ds(0, 3)], ps)):
        copy(ref, ref, sem.at[0], sem.at[0], d_c).wait_send()


def per_device(acts, grads, basis_in, basis_out):
    rows, feats = acts.shape
    kb = basis_in.shape[1]
    depth, kg = basis_out.shape
    dma = pltpu.SemaphoreType.DMA
    return pl.pallas_call(
        kernel,
        out_shape=jax.ShapeDtypeStruct((kg, kb), F32),
        in_specs=[pl.BlockSpec(memory_space=pl.ANY)] * 4,
        out_specs=pl.BlockSpec(memory_space=pltpu.VMEM),
        scratch_shapes=[
            pltpu.VMEM((4, 4, 2, rows // 4, feats), BF),
            pltpu.VMEM((feats, 2 * kb), BF),
            pltpu.VMEM((4, rows // 2, 4 * depth), BF),
            pltpu.VMEM((4 * depth, 2 * kg), BF),
            pltpu.VMEM((2, 2, rows // 2, kb), F32),
            pltpu.VMEM((4, 4, 2, rows // 2, kb), BF),
            pltpu.VMEM((4, 4, 2, rows // 8, kb), F32),
            pltpu.VMEM((3, 4, 4, 2, rows // 8, kb), BF),
            pltpu.VMEM((2, 4, 2, rows // 8, kb), BF),
            pltpu.VMEM((2, 4, 2, rows // 8, kb), BF),
            pltpu.VMEM((2, 2, 4, 4, rows // 8, kb), BF),
            pltpu.VMEM((4, 2, rows // 2, kg), BF),
            pltpu.VMEM((4, 2, rows // 2, kg), F32),
            pltpu.VMEM((3, 2, rows // 2, kg), BF),
            pltpu.VMEM((2, 2, 4, 2, rows // 4, kg), BF),
            pltpu.VMEM((6, kg // 2, kb), BF),
            pltpu.VMEM((6, kg // 2, kb), BF),
            pltpu.VMEM((2, kg // 2, kb), F32),
            dma((7,)),
            dma((48,)), dma((48,)),
            dma((1,)), dma((9, 2)),
            dma((1,)), dma((9,)),
            dma((1,)), dma((9,)),
            dma((3,)), dma((3,)),
            dma((3,)), dma((3,)),
            dma((6,)), dma((6,)),
        ],
        compiler_params=pltpu.CompilerParams(
            collective_id=0, has_side_effects=True, vmem_limit_bytes=58 * 2**20
        ),
        cost_estimate=pl.CostEstimate(flops=14 * 10**9, bytes_accessed=7 * 10**6, transcendentals=0),
    )(acts, basis_in, grads, basis_out)


def solution(mesh):
    in_specs = (P("col", "row"), P("row", "col"), P("row", "col"), P("col", "row"))
    return jax.shard_map(
        per_device, mesh=mesh, in_specs=in_specs, out_specs=P("row", "col"), check_vma=False
    )
```

```python
import jax
import jax.numpy as jnp
from jax import lax
from jax.experimental import pallas as pl
from jax.experimental.pallas import tpu as pltpu
from jax.sharding import PartitionSpec as P

BF = jnp.bfloat16
F32 = jnp.float32
MESH = pl.DeviceIdType.MESH
OWN, FIRST, REST = (0, 0, 384), (1, 0, 256), (1, 256, 128)
PIECES = (OWN, FIRST, REST)
TOP, LOW, THIRD, FOURTH, ALL = (0, 2), (2, 2), (2, 1), (3, 1), (0, 4)
MESSAGES = {TOP: [TOP], LOW: [THIRD, FOURTH], THIRD: [THIRD], FOURTH: [FOURTH], ALL: [TOP, THIRD, FOURTH]}
NEAR = {(0, 0): 0, (0, 1): 1, (0, 2): 4, (2, 0): 2, (2, 1): 3, (2, 2): 4}
FAR = {(0, 0): 6, (0, 1): 5, (0, 2): 5, (2, 0): 8, (2, 1): 7, (2, 2): 7}

ACTS = (2, 3, 5, 6, 7, 8, 9, 10, 15, 16, 17, 18, 20, 21, 22, 23, 29, 31, 33, 35, 37, 38, 39, 40)
HANDED = (28, 30, 32, 34)
OTHERS = [i for i in range(48) if i not in ACTS + HANDED]


def kernel(
    a, b, g, h, out,
    abuf, bbuf, gbuf, hbuf,
    cf, stg, acc, rx, lst, lrx, pin,
    zst, zall, zrx, pout,
    est, erx, esum,
    loc, ss, rs, xs, xr, ls, lr, ps, pr, gs, gr, zs, zr, es, er,
):
    row, col = lax.axis_index("row"), lax.axis_index("col")
    lo, x = row // 4, row % 4
    c, z, hi = col % 2, (col // 2) % 4, col // 8
    z0 = z % 2
    rows, feats = a.shape
    qr = rows // 4
    xrows = 2 * qr // 4
    depth, kg = h.shape
    kb = b.shape[1]

    def dev(x=x, lo=lo, hi=hi, z=z, c=c):
        return (lo * 4 + x, (hi * 4 + z) * 2 + c)

    d_y = dev(hi=1 - hi)
    d_z = dev(z=z + 1 - 2 * z0)
    d_q = dev(z=3 - z)
    d_c = dev(c=1 - c)
    d_yc = dev(hi=1 - hi, c=1 - c)
    d_l = dev(lo=1 - lo)
    d_b = dev(lo=1 - lo, hi=1 - hi)
    d_x = [dev(x=(x + r) % 4) for r in (1, 2, 3)]
    d_zs = [dev(z=(z + r) % 4) for r in (1, 2, 3)]

    pending = []

    def copy(src, dst, send, recv, to):
        return pltpu.make_async_remote_copy(
            src_ref=src, dst_ref=dst, send_sem=send, recv_sem=recv, device_id=to, device_id_type=MESH
        )

    def start(cp):
        cp.start()
        pending.append(cp)

    def send(src, dst, i, to):
        if i in OTHERS:
            start(copy(src, dst, ss.at[2 + OTHERS.index(i)], rs.at[i], to))
        else:
            copy(src, dst, ss.at[int(i in HANDED)], rs.at[i], to).start()

    def pass_on(ref, i, to):
        send(ref, ref, i, to)

    def got(dst, i):
        copy(dst, dst, ss.at[0], rs.at[i], d_c).wait_recv()

    def span(i, n):
        return pl.ds(pl.multiple_of(i * n, n), n)

    s_o = hi * 2 + z0
    s_y = (1 - hi) * 2 + z0
    s_z = hi * 2 + 1 - z0
    s_d = (1 - hi) * 2 + 1 - z0
    here, there = hi * 2 + c, (1 - hi) * 2 + c
    here_c, there_c = hi * 2 + 1 - c, (1 - hi) * 2 + 1 - c
    own_k, other_k = pl.ds(0, kg), pl.ds(kg, kg)

    def h_at(i, k):
        return hbuf.at[span(i, depth), k]

    l_a = [pltpu.make_async_copy(a.at[pl.ds(k * qr, qr)], abuf.at[s_o, k, c], loc.at[k]) for k in range(4)]
    l_b = pltpu.make_async_copy(b, bbuf.at[:, pl.ds(0, kb)], loc.at[4])
    l_g = pltpu.make_async_copy(g.at[span(c * 2 + hi, rows // 2)], gbuf.at[x, :, span(here, depth)], loc.at[5])
    l_h = pltpu.make_async_copy(h, h_at(here, own_k), loc.at[6])
    for cp in (*l_a, l_b, l_g, l_h):
        cp.start()

    barrier = pltpu.get_barrier_semaphore()
    friends = [d_y, d_c, d_yc, d_l, d_b] + d_x + d_zs
    for to in friends:
        pl.semaphore_signal(barrier, inc=1, device_id=to, device_id_type=MESH)
    pl.semaphore_wait(barrier, len(friends))

    def send_g(i, hh, cc, to):
        send(g.at[span(cc * 2 + hh, rows // 2)], gbuf.at[x, :, span(here, depth)], i, to)

    def send_a(k, i, to):
        send(a.at[pl.ds(k * qr, qr)], abuf.at[s_o, k, c], i, to)

    def b_at(piece):
        return bbuf.at[:, pl.ds(kb + piece[1], piece[2])]

    def send_b(piece, i):
        send(b.at[:, pl.ds(piece[1], piece[2])], b_at(piece), i, d_q)

    send_g(0, 1 - hi, c, d_y)
    send_g(1, 1 - hi, 1 - c, d_yc)
    send_a(0, 2, d_y)
    send_a(2, 3, d_z)
    send_b(FIRST, 4)
    send_a(1, 5, d_y)
    send_a(3, 6, d_z)
    for k in range(4):
        send_a(k, 7 + k, d_c)
    send_g(11, hi, 1 - c, d_c)
    send(h, h_at(here, own_k), 14, d_c)
    send_a(2, 15, d_y)
    send_a(0, 16, d_z)
    send_a(3, 17, d_y)
    send_a(1, 18, d_z)
    send(h, h_at(here, other_k), 12, d_l)
    send(h, h_at(here, other_k), 13, d_b)
    send_b(REST, 19)

    def x_copy(s, q, ch, r):
        pb, c0, w = PIECES[ch]
        qs, cs = pl.ds(*q), pl.ds(c0, w)
        key = (0 if q[0] == 0 else 2, ch)
        piece = jnp.where(s % 2 == z0, NEAR[key], FAR[key])
        return copy(
            stg.at[s, qs, pb, span((x + r) % 4, xrows), cs], rx.at[r - 1, s, qs, pb, :, cs],
            xs.at[0], xr.at[piece, s // 2], d_x[r - 1],
        )

    def block(s, q, *chunks):
        qs = pl.ds(*q)
        c0 = PIECES[chunks[0]][0] * kb + PIECES[chunks[0]][1]
        w = sum(PIECES[ch][2] for ch in chunks)
        lhs = abuf[s, qs].reshape(q[1] * 2 * qr, feats)
        part = jnp.dot(lhs, bbuf[:, pl.ds(c0, w)], preferred_element_type=F32)
        for ch in chunks:
            pb, first, width = PIECES[ch]
            cut = part[:, pb * kb + first - c0:][:, :width].reshape(q[1], 2 * qr, width)
            cf[pl.ds(0, q[1]), pb, :, pl.ds(first, width)] = cut
            stg[s, qs, pb, :, pl.ds(first, width)] = cut.astype(BF)
        for ch in chunks:
            for m in MESSAGES[q]:
                for r in (1, 2, 3):
                    x_copy(s, m, ch, r).start()
        for ch in chunks:
            pb, first, width = PIECES[ch]
            cs = pl.ds(first, width)
            acc[s, qs, pb, :, cs] = cf[pl.ds(0, q[1]), pb, span(x, xrows), cs]

    def span_of(chunks):
        return PIECES[chunks[0]][0], pl.ds(PIECES[chunks[0]][1], sum(PIECES[ch][2] for ch in chunks))

    def add_x(i, zz, q, *chunks):
        qs = pl.ds(*q)
        pb, cs = span_of(chunks)
        for hh in (1 - lo, lo):
            s = hh * 2 + zz
            ref = rx.at[:, s, qs, pb, :, cs]
            copy(ref, ref, xs.at[0], xr.at[i, hh], d_c).wait_recv()
            total = acc[s, qs, pb, :, cs]
            for r in range(3):
                total = total + rx[r, s, qs, pb, :, cs].astype(F32)
            if hh is lo:
                acc[s, qs, pb, :, cs] = total
            else:
                ref = lst.at[zz, qs, pb, :, cs]
                ref[...] = total.astype(lst.dtype)
                copy(ref, lrx.at[zz, qs, pb, :, cs], ls.at[0], lr.at[i], d_l).start()

    def add_y(i, zz, q, *chunks):
        qs = pl.ds(*q)
        pb, cs = span_of(chunks)
        ref = lrx.at[zz, qs, pb, :, cs]
        copy(ref, ref, ls.at[0], lr.at[i], d_c).wait_recv()
        pin[pb, zz, qs, x, :, cs] = (acc[lo * 2 + zz, qs, pb, :, cs] + lrx[zz, qs, pb, :, cs].astype(F32)).astype(BF)
        for r in (1, 2, 3):
            ref = pin.at[pb, zz, qs, x, :, cs]
            copy(ref, ref, ps.at[0], pr.at[i], d_x[r - 1]).start()

    def gathered(i, zz, q, *chunks):
        pb, cs = span_of(chunks)
        ref = pin.at[pb, zz, pl.ds(*q), pl.ds(0, 3), :, cs]
        copy(ref, ref, ps.at[0], pr.at[i], d_c).wait_recv()

    for cp in l_a:
        cp.wait()
    l_b.wait()
    for k in range(4):
        got(abuf.at[s_o, k, 1 - c], 7 + k)
    block(s_o, TOP, 0)
    block(s_o, LOW, 0)

    l_g.wait()
    got(gbuf.at[x, :, span(here_c, depth)], 11)
    got(gbuf.at[x, :, span(there, depth)], 0)
    got(gbuf.at[x, :, span(there_c, depth)], 1)
    for r in (1, 2, 3):
        copy(gbuf.at[x], gbuf.at[x], gs.at[0], gr.at[0], d_x[r - 1]).start()

    got(abuf.at[s_z, 2, c], 3)
    pass_on(abuf.at[s_z, 2, c], 20, d_c)
    got(abuf.at[s_z, 3, c], 6)
    pass_on(abuf.at[s_z, 3, c], 21, d_c)
    got(abuf.at[s_y, 0, c], 2)
    pass_on(abuf.at[s_y, 0, c], 22, d_c)
    got(abuf.at[s_z, 2, 1 - c], 20)
    got(abuf.at[s_z, 3, 1 - c], 21)
    block(s_z, LOW, 0)
    got(abuf.at[s_y, 1, c], 5)
    pass_on(abuf.at[s_y, 1, c], 23, d_c)
    got(abuf.at[s_y, 0, 1 - c], 22)
    got(abuf.at[s_y, 1, 1 - c], 23)
    block(s_y, TOP, 0)

    got(abuf.at[s_z, 0, c], 16)
    pass_on(abuf.at[s_y, 0, c], 28, d_z)
    pass_on(abuf.at[s_z, 0, c], 29, d_c)
    got(b_at(FIRST), 4)
    got(abuf.at[s_z, 1, c], 18)
    pass_on(abuf.at[s_y, 1, c], 30, d_z)
    pass_on(abuf.at[s_z, 1, c], 31, d_c)
    block(s_o, TOP, 1)
    block(s_y, TOP, 1)
    got(abuf.at[s_z, 0, 1 - c], 29)
    got(abuf.at[s_z, 1, 1 - c], 31)
    block(s_z, TOP, 0)
    block(s_o, LOW, 1)
    got(abuf.at[s_y, 2, c], 15)
    pass_on(abuf.at[s_y, 2, c], 33, d_c)

    third_z = copy(abuf.at[s_y, 2, c], abuf.at[s_y, 2, c], ss.at[1], rs.at[32], d_z)
    third_y = copy(abuf.at[s_z, 2, c], abuf.at[s_z, 2, c], ss.at[1], rs.at[32], d_y)

    @pl.when(c == 0)
    def _():
        third_z.start()

    add_x(0, z0, TOP, 0)
    add_x(1, z0, TOP, 1)
    got(abuf.at[s_y, 3, c], 17)
    pass_on(abuf.at[s_y, 3, c], 35, d_c)
    block(s_z, TOP, 1)
    got(abuf.at[s_y, 2, 1 - c], 33)
    got(abuf.at[s_y, 3, 1 - c], 35)
    block(s_y, LOW, 0, 1)
    block(s_z, LOW, 1)

    h2 = depth // 2
    got(h_at(here, other_k), 12)
    send(hbuf.at[span(here * 2, h2), other_k], hbuf.at[span(here * 2, h2), own_k], 24, d_b)
    got(h_at(there, other_k), 13)
    send(hbuf.at[span(there * 2 + 1, h2), other_k], hbuf.at[span(there * 2 + 1, h2), own_k], 26, d_l)
    pass_on(h_at(here, other_k), 25, d_c)
    pass_on(h_at(there, other_k), 27, d_c)
    add_x(2, z0, LOW, 0)
    add_x(3, z0, LOW, 1)
    pass_on(abuf.at[s_z, 3, c], 34, d_y)
    add_y(0, z0, TOP, 0)
    add_y(1, z0, TOP, 1)

    got(hbuf.at[span(there * 2, h2), own_k], 24)
    got(hbuf.at[span(there * 2 + 1, h2), own_k], 26)
    pass_on(h_at(there, own_k), 36, d_c)
    l_h.wait()
    got(h_at(here_c, own_k), 14)
    got(h_at(here_c, other_k), 25)
    got(h_at(there_c, other_k), 27)
    three = gbuf.at[pl.ds(0, 3)]
    copy(three, three, gs.at[0], gr.at[0], d_c).wait_recv()
    got(h_at(there_c, own_k), 36)
    part = jnp.dot(gbuf[...].reshape(2 * rows, 4 * depth), hbuf[...], preferred_element_type=F32)
    for k in (0, 1):
        cut = part[:, k * kg:][:, :kg].reshape(4, rows // 2, kg)
        zall[:, k] = cut
        zst[:, k] = cut.astype(zst.dtype)
    for r in (1, 2, 3):
        copy(zst.at[(z + r) % 4], zrx.at[r - 1], zs.at[0], zr.at[0], d_zs[r - 1]).start()
    add_y(2, z0, LOW, 0)
    add_y(3, z0, LOW, 1)

    got(b_at(REST), 19)

    @pl.loop(0, 3)
    def _(j):
        s = jnp.where(j == 0, s_o, jnp.where(j == 1, s_z, s_y))
        block(s, TOP, 2)
        block(s, LOW, 2)

    got(abuf.at[s_d, 0, c], 28)
    pass_on(abuf.at[s_d, 0, c], 37, d_c)
    got(abuf.at[s_d, 1, c], 30)
    pass_on(abuf.at[s_d, 1, c], 38, d_c)

    @pl.when(c == 1)
    def _():
        third_y.start()

    got(abuf.at[s_d, 0, 1 - c], 37)
    got(abuf.at[s_d, 1, 1 - c], 38)
    block(s_d, TOP, 0, 1, 2)
    add_x(4, z0, ALL, 2)

    mine, theirs = span(hi, 2), span(1 - hi, 2)
    copy(zrx, zrx, zs.at[0], zr.at[0], d_c).wait_recv()
    for k in (0, 1):
        total = zall[z, k] + zrx[0, k].astype(F32) + zrx[1, k].astype(F32) + zrx[2, k].astype(F32)
        pout[k, z0, mine, c] = total.astype(BF).reshape(2, qr, kg)
    pass_on(pout.at[:, z0, mine, c], 41, d_y)
    pass_on(pout.at[:, z0, mine, c], 45, d_z)
    pass_on(pout.at[:, z0, mine, c], 43, d_c)

    got(abuf.at[s_d, 3, c], 34)
    pass_on(abuf.at[s_d, 3, c], 40, d_c)
    got(abuf.at[s_d, 2, c], 32)
    pass_on(abuf.at[s_d, 2, c], 39, d_c)
    got(abuf.at[s_d, 3, 1 - c], 40)
    block(s_d, FOURTH, 0, 1, 2)
    add_x(5, 1 - z0, TOP, 1, 2)
    add_x(6, 1 - z0, TOP, 0)
    got(abuf.at[s_d, 2, 1 - c], 39)
    block(s_d, THIRD, 0, 1, 2)

    add_y(4, z0, ALL, 2)
    got(pout.at[:, z0, theirs, c], 41)
    pass_on(pout.at[:, z0, theirs, c], 42, d_z)
    pass_on(pout.at[:, z0, theirs, c], 46, d_c)
    add_y(5, 1 - z0, TOP, 1, 2)
    add_y(6, 1 - z0, TOP, 0)
    got(pout.at[:, 1 - z0, mine, c], 45)
    pass_on(pout.at[:, 1 - z0, mine, c], 44, d_c)
    add_x(7, 1 - z0, LOW, 1, 2)
    add_x(8, 1 - z0, LOW, 0)
    got(pout.at[:, 1 - z0, theirs, c], 42)
    pass_on(pout.at[:, 1 - z0, theirs, c], 47, d_c)
    add_y(7, 1 - z0, LOW, 1, 2)
    add_y(8, 1 - z0, LOW, 0)

    got(pout.at[:, z0, mine, 1 - c], 43)
    got(pout.at[:, z0, theirs, 1 - c], 46)
    got(pout.at[:, 1 - z0, mine, 1 - c], 44)
    got(pout.at[:, 1 - z0, theirs, 1 - c], 47)

    def squares(k, pb):
        left = pout[k].reshape(4 * rows, kg)
        right = pin[pb].reshape(4 * rows, kb)
        t = lax.dot_general(left, right, (((0,), (0,)), ((), ())), preferred_element_type=F32)
        return t * t

    hk = kg // 2
    upper, lower = pl.ds(0, hk), pl.ds(hk, hk)

    def e_copy(i, to):
        return copy(est.at[i], erx.at[i], es.at[0], er.at[i], to)

    def give(i, values, to):
        est[i] = values.astype(est.dtype)
        e_copy(i, to).start()

    def taken(i):
        e_copy(i, d_c).wait_recv()
        return erx[i].astype(F32)

    gathered(1, z0, TOP, 1)
    gathered(3, z0, LOW, 1)
    gathered(4, z0, ALL, 2)
    gathered(5, 1 - z0, TOP, 1, 2)
    gathered(7, 1 - z0, LOW, 1, 2)
    quad = squares(1, 1)
    give(0, quad[:hk], d_l)
    give(1, quad[hk:], d_q)
    quad = squares(0, 1)
    esum[0] = quad[:hk]
    give(2, quad[hk:], d_q)
    gathered(0, z0, TOP, 0)
    gathered(2, z0, LOW, 0)
    gathered(6, 1 - z0, TOP, 0)
    gathered(8, 1 - z0, LOW, 0)
    quad = squares(1, 0)
    esum[1] = quad[hk:]
    give(3, quad[:hk], d_l)
    give(4, esum[0] + taken(0), d_q)
    give(5, esum[1] + taken(1), d_l)
    total = squares(0, 0)
    out[lower] = total[hk:]
    out[upper] = total[:hk] + taken(3)
    out[lower] = out[lower] + taken(2)
    out[upper] = (out[upper] + taken(4)) * 0.25
    out[lower] = (out[lower] + taken(5)) * 0.25

    for cp in pending:
        cp.wait_send()

    handed = abuf.at[0, pl.ds(0, 2)]
    copy(handed, handed, ss.at[1], rs.at[32], d_c).wait_send()
    sent = abuf.at[pl.ds(0, 3)]
    copy(sent, sent, ss.at[0], rs.at[32], d_c).wait_send()

    for ref, sem in ((stg.at[:, :, :, pl.ds(0, 3 * xrows)], xs), (lst, ls), (pin.at[:, :, :, pl.ds(0, 3)], ps), (three, gs), (zst.at[pl.ds(0, 3)], zs), (est, es)):
        copy(ref, ref, sem.at[0], sem.at[0], d_c).wait_send()


def per_device(acts, grads, basis_in, basis_out):
    rows, feats = acts.shape
    kb = basis_in.shape[1]
    depth, kg = basis_out.shape
    dma = pltpu.SemaphoreType.DMA
    return pl.pallas_call(
        kernel,
        out_shape=jax.ShapeDtypeStruct((kg, kb), F32),
        in_specs=[pl.BlockSpec(memory_space=pl.ANY)] * 4,
        out_specs=pl.BlockSpec(memory_space=pltpu.VMEM),
        scratch_shapes=[
            pltpu.VMEM((4, 4, 2, rows // 4, feats), BF),
            pltpu.VMEM((feats, 2 * kb), BF),
            pltpu.VMEM((4, rows // 2, 4 * depth), BF),
            pltpu.VMEM((4 * depth, 2 * kg), BF),
            pltpu.VMEM((2, 2, rows // 2, kb), F32),
            pltpu.VMEM((4, 4, 2, rows // 2, kb), BF),
            pltpu.VMEM((4, 4, 2, rows // 8, kb), F32),
            pltpu.VMEM((3, 4, 4, 2, rows // 8, kb), BF),
            pltpu.VMEM((2, 4, 2, rows // 8, kb), BF),
            pltpu.VMEM((2, 4, 2, rows // 8, kb), BF),
            pltpu.VMEM((2, 2, 4, 4, rows // 8, kb), BF),
            pltpu.VMEM((4, 2, rows // 2, kg), BF),
            pltpu.VMEM((4, 2, rows // 2, kg), F32),
            pltpu.VMEM((3, 2, rows // 2, kg), BF),
            pltpu.VMEM((2, 2, 4, 2, rows // 4, kg), BF),
            pltpu.VMEM((6, kg // 2, kb), BF),
            pltpu.VMEM((6, kg // 2, kb), BF),
            pltpu.VMEM((2, kg // 2, kb), F32),
            dma((7,)),
            dma((2 + len(OTHERS),)), dma((48,)),
            dma((1,)), dma((9, 2)),
            dma((1,)), dma((9,)),
            dma((1,)), dma((9,)),
            dma((1,)), dma((1,)),
            dma((1,)), dma((1,)),
            dma((1,)), dma((6,)),
        ],
        compiler_params=pltpu.CompilerParams(
            collective_id=0, has_side_effects=True, vmem_limit_bytes=58 * 2**20
        ),
        cost_estimate=pl.CostEstimate(flops=14 * 10**9, bytes_accessed=7 * 10**6, transcendentals=0),
    )(acts, basis_in, grads, basis_out)


def solution(mesh):
    in_specs = (P("col", "row"), P("row", "col"), P("row", "col"), P("col", "row"))
    return jax.shard_map(
        per_device, mesh=mesh, in_specs=in_specs, out_specs=P("row", "col"), check_vma=False
    )
```
